32 devices in a mesh: dp: 16 (over z, x, core), mp: 2 (over y).
Axes of the slice: x: 2, y: 2, z: 4, core: 2. Of those that a mesh axis runs over, the one named last changes fastest.
Arguments:
- layer_input: float32 [4096, 512], P('dp'), may hold values from -6 to 6
- grad_out: float32 [4096, 512], P('dp'), may hold values from -6 to 6
- segment: int32 [16, 256], P('dp'), may hold values from 0 to 7, never falling along the last dimension, each value on 1 to 128 neighbouring positions
- item_ids: int32 [4096], P('dp'), may hold values from 0 to 31
- w_uvqk: float32 [512, 2048], P(None, 'mp'), may hold values from -0.25 to 0.25
- w_out: float32 [512, 512], P('mp'), may hold values from -0.25 to 0.25
- table: float32 [32, 512], P(('dp', 'mp')), may hold values from -6 to 6
- accum: float32 [32], P(('dp', 'mp')), may hold values from 0.1 to 2
Outputs:
- w_uvqk_grad: float32 [512, 2048], P(None, 'mp')
- w_out_grad: float32 [512, 512], P('mp')
- new_table: float32 [32, 512], P(('dp', 'mp'))
- new_accum: float32 [32], P(('dp', 'mp'))
The draws below stay inside these ranges and needn't reach their ends.
Inputs may be any that keep to these rules, and one draw needn't show every extreme that they name: `segment`: segment numbers never fall along a row; a history holds at most 128 tokens and some history holds exactly that many.
All inputs are finite; a program needn't handle non-finite values.
Results may differ from the reference program's by a relative error of at most 0.0003.
Values sent between devices are 32-bit elements; how exact they have to be, the bound alone decides.
A program may use at most 64 MiB of HBM per device.

```python
import math
import jax
import jax.numpy as jnp
import numpy as np
from jax import lax

D = 512
HEADS = 8
HEAD_DIM = 64
TOK_DEV = 256
SEQ_DEV = 8
SEQ_MOST = 128
TOKENS = 4096
ROWS = 32
N_DP = 16


def plant(array, own_key, low, high):
    spot = [jax.random.randint(jax.random.fold_in(own_key, axis), (), 0, length) for axis, length in enumerate(array.shape)]
    main_axis = array.shape.index(max(array.shape))
    next_to = spot[:main_axis] + [(spot[main_axis] + 1) % array.shape[main_axis]] + spot[main_axis + 1:]
    return array.at[tuple(spot)].set(low).at[tuple(next_to)].set(high)


def steps_of(stream_key, dims, cuts, low, high):
    def one(dim, parts):
        draws = jax.random.uniform(jax.random.fold_in(jax.random.fold_in(stream_key, 6), dim), (parts,), jnp.float32, low / len(cuts), high / len(cuts))
        return jnp.repeat(jnp.exp(draws), dims[dim] // parts).reshape((-1,) + (1,) * (len(dims) - dim - 1))

    factor_of = one(*cuts[0])
    for cut in cuts[1:]:
        factor_of = factor_of * one(*cut)
    return factor_of


def rank_table(number_of, skew):
    weights = [(1 << 20) // math.isqrt(standing ** skew) + 1 for standing in range(1, number_of + 1)]
    spread = 1 + sum(weights) // (1 << 30)
    return np.cumsum(np.array([max(1, weight // spread) for weight in weights]))


def ranked_ids(own_key, extent, number_of, skew):
    grid = rank_table(number_of, skew)
    ticket = jax.random.randint(jax.random.fold_in(own_key, 1), extent, 0, int(grid[number_of - 1]))
    grade = jnp.searchsorted(jnp.asarray(grid, jnp.int32), ticket, side="right")
    return jax.random.permutation(jax.random.fold_in(own_key, 2), number_of)[grade].astype(jnp.int32)


def profile(amount, total, reach, skew):
    loads = [(1 << 20) // math.isqrt(standing ** skew) + 1 for standing in range(2, amount + 1)]
    surplus, given = total - reach - (amount - 1), [1] * (amount - 1)
    while surplus > 0:
        candidates = [i for i in range(amount - 1) if given[i] < reach]
        pool, remaining = sum([loads[i] for i in candidates]), surplus
        for i in candidates:
            more = min(reach - given[i], max(1, remaining * loads[i] // pool), surplus)
            given[i] = given[i] + more
            surplus = surplus - more
    return np.array([reach] + given)


def uneven(key, number_of, total, limit, lean):
    if number_of == 2:
        one = jax.random.randint(key, (), max(1, total - limit), min(limit, total - 1) + 1)
        return jnp.stack([one, total - one])
    tallies = jnp.asarray(profile(number_of, total, limit, lean), jnp.int32)
    pairs = (number_of - 1) // 2
    giver, sink = tallies[1:1 + 2 * pairs:2], tallies[2:2 + 2 * pairs:2]
    margin = jnp.minimum(giver - 1, limit - sink)
    moved = jax.random.randint(jax.random.fold_in(key, 1), (pairs,), 0, 1 << 20) % (margin + 1)
    tallies = tallies.at[1:1 + 2 * pairs:2].set(giver - moved).at[2:2 + 2 * pairs:2].set(sink + moved)
    return tallies[jax.random.permutation(jax.random.fold_in(key, 2), number_of)]


def normal_values(stream_key, extent, spread, most, cuts=(), dtype=jnp.bfloat16):
    entries = spread * jax.random.normal(stream_key, extent, jnp.float32)
    if cuts:
        entries = entries * steps_of(stream_key, extent, cuts, -0.22, 0.18)
    return jnp.clip(entries, -most, most).astype(dtype)


def setup_inputs(seed: int = 0) -> dict:
    seeds = jax.random.split(jax.random.key(seed), 9)
    return {
        "layer_input": normal_values(seeds[0], (TOKENS, D), 1.0, 6.0, ((0, 16),), jnp.float32),
        "grad_out": normal_values(seeds[1], (TOKENS, D), 1.0, 6.0, ((0, 16),), jnp.float32),
        "segment": jax.vmap(lambda own: jnp.searchsorted(jnp.cumsum(uneven(own, SEQ_DEV, TOK_DEV, SEQ_MOST, 2)), jnp.arange(TOK_DEV), side="right"))(jax.random.split(seeds[2], N_DP)).reshape((N_DP, TOK_DEV)).astype(jnp.int32),
        "item_ids": plant(ranked_ids(seeds[3], (TOKENS,), ROWS, 2), jax.random.fold_in(seeds[3], 3), 0, ROWS - 1).astype(jnp.int32),
        "w_uvqk": normal_values(seeds[4], (D, 4 * D), D ** -0.5, 0.25, ((1, 2),), jnp.float32),
        "w_out": normal_values(seeds[5], (D, D), D ** -0.5, 0.25, ((0, 2),), jnp.float32),
        "table": normal_values(seeds[6], (ROWS, D), 1.0, 6.0, ((0, 32),), jnp.float32),
        "accum": jnp.clip(jnp.exp(math.log(2.0) - 2.9957323 * jax.random.uniform(seeds[7], (ROWS,), jnp.float32) ** steps_of(seeds[7], (ROWS,), ((0, 32),), -0.2, 0.2)), 0.1, 2.0),
    }


highest = lax.Precision.HIGHEST

def mdot(left, right):
    return jnp.dot(left, right, precision=highest, preferred_element_type=jnp.float32)

def group_grads(layer_input, grad_out, segment, w_uvqk, w_out):
    count = layer_input.shape[0]
    scale = HEAD_DIM ** (-0.5)
    pre = mdot(layer_input, w_uvqk).reshape(count, HEADS, 4, HEAD_DIM)
    act = jax.nn.silu(pre)
    ublk, vblk, qblk, kblk = (act[:, :, 0], act[:, :, 1], act[:, :, 2], act[:, :, 3])
    place = jnp.arange(count)
    mask = ((segment[:, None] == segment[None, :]) & (place[:, None] >= place[None, :])).astype(jnp.float32)
    score = jnp.einsum('ihd,jhd->hij', qblk, kblk, precision=highest) * scale
    sigm = jax.nn.sigmoid(score)
    attn = score * sigm * mask
    outv = jnp.einsum('hij,jhd->ihd', attn, vblk, precision=highest).reshape(count, D)
    mean = lax.optimization_barrier(jnp.sum(outv, axis=1, keepdims=True)) / D
    var = lax.optimization_barrier(jnp.sum(outv * outv, axis=1, keepdims=True)) / D - mean * mean
    rstd = lax.rsqrt(var + 1e-05)
    normed = (outv - mean) * rstd
    nheads = normed.reshape(count, HEADS, HEAD_DIM)
    zval = (nheads * ublk).reshape(count, D)
    dzval = mdot(grad_out, w_out.T).reshape(count, HEADS, HEAD_DIM)
    w_out_grad = mdot(zval.T, grad_out)
    dnorm = (dzval * ublk).reshape(count, D)
    dublk = dzval * nheads
    first = lax.optimization_barrier(jnp.sum(dnorm, axis=1, keepdims=True)) / D
    second = lax.optimization_barrier(jnp.sum(dnorm * normed, axis=1, keepdims=True)) / D
    dout = (rstd * (dnorm - first - normed * second)).reshape(count, HEADS, HEAD_DIM)
    dattn = jnp.einsum('ihd,jhd->hij', dout, vblk, precision=highest)
    dvblk = jnp.einsum('hij,ihd->jhd', attn, dout, precision=highest)
    dscore = dattn * mask * (sigm * (1.0 + score * (1.0 - sigm))) * scale
    dqblk = jnp.einsum('hij,jhd->ihd', dscore, kblk, precision=highest)
    dkblk = jnp.einsum('hij,ihd->jhd', dscore, qblk, precision=highest)
    dact = jnp.stack([dublk, dvblk, dqblk, dkblk], axis=2)
    psig = jax.nn.sigmoid(pre)
    dpre = (dact * psig * (1.0 + pre * (1.0 - psig))).reshape(count, 4 * D)
    w_uvqk_grad = mdot(layer_input.T, dpre)
    x_grad = grad_out + mdot(dpre, w_uvqk.T)
    return (w_uvqk_grad, w_out_grad, x_grad)

def reference(layer_input, grad_out, segment, item_ids, w_uvqk, w_out, table, accum):
    groups = segment.shape[0]
    inputs = layer_input.reshape(groups, TOK_DEV, D)
    cotans = grad_out.reshape(groups, TOK_DEV, D)

    def step(carry, pieces):
        one, two, three = group_grads(pieces[0], pieces[1], pieces[2], w_uvqk, w_out)
        return ((carry[0] + one, carry[1] + two), three)
    start = (jnp.zeros((D, 4 * D), jnp.float32), jnp.zeros((D, D), jnp.float32))
    totals, x_grads = lax.scan(step, start, (inputs, cotans, segment))
    x_grad = x_grads.reshape(groups * TOK_DEV, D)
    row_grad = jax.ops.segment_sum(x_grad, item_ids, num_segments=ROWS)
    new_accum = accum + lax.optimization_barrier(jnp.sum(row_grad * row_grad, axis=1)) / D
    new_table = table - 0.5 * row_grad * lax.rsqrt(new_accum)[:, None]
    return (totals[0], totals[1], new_table, new_accum)
```

```python
import functools

import jax
import jax.numpy as jnp
from jax import lax
from jax.experimental import pallas as pl
from jax.experimental.pallas import tpu as pltpu
from jax.sharding import PartitionSpec as P

HEAD_DIM = 64
BLOCK = 4 * HEAD_DIM
MESH = pl.DeviceIdType.MESH
F32, BF16 = jnp.float32, jnp.bfloat16

NN = (((1,), (0,)), ((), ()))
NT = (((1,), (1,)), ((), ()))
TN = (((0,), (0,)), ((), ()))


def halves(value):
    high = value.astype(BF16)
    return high, (value - high.astype(F32)).astype(BF16)


def dot(left, right, dims):
    return lax.dot_general(left, right, dims, preferred_element_type=F32)


def dot3(left, right, dims):
    return dot(left[0], right[1], dims) + dot(left[1], right[0], dims) + dot(left[0], right[0], dims)


def kernel(
    n_z, n_mp, fuse,
    x_ref, g_ref, seg_ref, ids_ref, w_ref, wo_ref, table_ref, accum_ref,
    out, wopart_ref, newt_ref, newa_ref,
    buf, xt_hi, xt_lo, act, dsilu, attn, dsfac, outv, dzs, stat, stat_in,
    rc, rx, rz, sl, slc, slx, slz, slq, slm,
    ps, pr, zs, zr, ls, lr, lzs, lzr, ms, mr,
):
    count, width = x_ref.shape
    heads = w_ref.shape[1] // BLOCK
    rows = sl.shape[0]
    own = table_ref.shape[0]
    off = 1 if fuse else 0
    pieces = heads + off
    half = buf.shape[1] // 2
    quarter = half // 2
    chunk = quarter // n_z
    scale = HEAD_DIM ** (-0.5)

    dp, mp = lax.axis_index("dp"), lax.axis_index("mp")
    z, x, c = dp // 4, (dp // 2) % 2, dp % 2
    at_core = {"dp": z * 4 + x * 2 + (1 - c)}
    at_x = {"dp": z * 4 + (1 - x) * 2 + c}
    z_of = [lax.rem(z + k, n_z) for k in range(1, n_z)]
    at_z = [{"dp": zz * 4 + x * 2 + c} for zz in z_of]
    at_mp = [{"mp": lax.rem(mp + k, n_mp)} for k in range(1, n_mp)]

    barrier = pltpu.get_barrier_semaphore()
    partners = [at_core, at_x] + at_z + at_mp
    for partner in partners:
        pl.semaphore_signal(barrier, inc=1, device_id=partner, device_id_type=MESH)

    def remote(src, dst, send, recv, where):
        return pltpu.make_async_remote_copy(
            src_ref=src, dst_ref=dst, send_sem=send, recv_sem=recv, device_id=where, device_id_type=MESH
        )

    def span(start, size):
        return pl.ds(pl.multiple_of(start, 8), size)

    mine = span(c * half, half)
    theirs = span((1 - c) * half, half)
    my_q = span(c * half + x * quarter, quarter)
    their_q = span(c * half + (1 - x) * quarter, quarter)
    my_chunk = span(c * half + x * quarter + z * chunk, chunk)

    def core_rs(p):
        return remote(buf.at[p, theirs], rc.at[p], ps.at[0, p], pr.at[0, p], at_core)

    def x_rs(p):
        return remote(buf.at[p, their_q], rx.at[p], ps.at[1, p], pr.at[1, p], at_x)

    def z_rs(p, k):
        part = span(c * half + x * quarter + z_of[k] * chunk, chunk)
        return remote(buf.at[p, part], rz.at[p, k], zs.at[0, p, k], zr.at[0, p, k], at_z[k])

    def z_ag(p, k):
        return remote(out.at[p, my_chunk], out.at[p, my_chunk], zs.at[1, p, k], zr.at[1, p, k], at_z[k])

    def x_ag(p):
        return remote(out.at[p, my_q], out.at[p, my_q], ps.at[2, p], pr.at[2, p], at_x)

    def core_ag(p):
        return remote(out.at[p, mine], out.at[p, mine], ps.at[3, p], pr.at[3, p], at_core)

    def stage(s, p):
        if s == 0:
            core_rs(p).start()
        elif s == 1:
            core_rs(p).wait()
            buf[p, their_q] += rc[p, span((1 - x) * quarter, quarter)]
            x_rs(p).start()
            buf[p, my_q] += rc[p, span(x * quarter, quarter)]
        elif s == 2:
            x_rs(p).wait()
            buf[p, my_q] += rx[p]
            for k in range(n_z - 1):
                z_rs(p, k).start()
        elif s == 3:
            total = buf[p, my_chunk]
            for k in range(n_z - 1):
                z_rs(p, k).wait()
                total = total + rz[p, k]
            out[p, my_chunk] = total
            for k in range(n_z - 1):
                z_ag(p, k).start()
        elif s == 4:
            for k in range(n_z - 1):
                z_ag(p, k).wait()
            x_ag(p).start()
        elif s == 5:
            x_ag(p).wait()
            core_ag(p).start()
        else:
            core_ag(p).wait()

    seg = jnp.broadcast_to(seg_ref[...].astype(F32), (count, count))
    spot = lax.broadcasted_iota(jnp.int32, (count, count), 0)
    other = lax.broadcasted_iota(jnp.int32, (count, count), 1)
    mask = jnp.where((seg == seg.T) & (spot >= other), 1.0, 0.0)
    xs = halves(x_ref[...])
    gs = halves(g_ref[...])

    def forward(h, sums):
        ws = halves(w_ref[:, pl.ds(pl.multiple_of(h * BLOCK, BLOCK), BLOCK)])
        pre = dot3(xs, ws, NN)
        sig = jax.nn.sigmoid(pre)
        val = pre * sig
        act[h] = val
        dsilu[h] = sig * (1.0 + pre * (1.0 - sig))
        u, v = val[:, 0:64], val[:, 64:128]
        q, k = val[:, 128:192], val[:, 192:256]
        score = dot3(halves(q), halves(k), NT) * scale
        ssig = jax.nn.sigmoid(score)
        a = score * ssig * mask
        attn[h] = a
        dsfac[h] = mask * (ssig * (1.0 + score * (1.0 - ssig))) * scale
        o = dot3(halves(a), halves(v), NN)
        outv[h] = o
        wos = halves(wo_ref[pl.ds(pl.multiple_of(h * HEAD_DIM, HEAD_DIM), HEAD_DIM), :])
        dz = dot3(gs, wos, NT)
        dzs[h] = dz
        dn = dz * u
        return (sums[0] + o, sums[1] + o * o, sums[2] + dn, sums[3] + dn * o)

    zero = jnp.zeros((count, HEAD_DIM), F32)
    sums = lax.fori_loop(0, heads, forward, (zero, zero, zero, zero))
    lane = lax.broadcasted_iota(jnp.int32, (count, 128), 1)
    packed = jnp.zeros((count, 128), F32)
    for i in range(4):
        packed = jnp.where(lane == i, jnp.sum(sums[i], axis=1, keepdims=True), packed)
    stat[...] = packed.T[0:8]
    pl.semaphore_wait(barrier, len(partners))

    def stat_to(k):
        return remote(stat, stat_in.at[k], ms.at[0, k], mr.at[0, k], at_mp[k])

    for k in range(n_mp - 1):
        stat_to(k).start()
    x_t = x_ref[...].T
    xt_hi[...], xt_lo[...] = halves(x_t)
    place = lax.broadcasted_iota(jnp.int32, (rows, count), 0)
    inner = n_z * n_mp * own
    pc, px = place // (2 * inner), (place // inner) % 2
    pz, pm = (place // (n_mp * own)) % n_z, place % (n_mp * own)
    wanted = ((pz * 2 + px) * 2 + pc) * (n_mp * own) + pm
    hits = jnp.where(wanted == ids_ref[...], 1.0, 0.0).astype(BF16)
    sl[...] = (dot(hits, gs[0], NN) + dot(hits, gs[1], NN)) * (1.0 / n_mp)

    total = stat[...]
    for k in range(n_mp - 1):
        stat_to(k).wait()
        total = total + stat_in[k]
    cols = jnp.concatenate([total, jnp.zeros((120, count), F32)], axis=0).T
    mean = cols[:, 0:1] / width
    var = cols[:, 1:2] / width - mean * mean
    rstd = lax.rsqrt(var + 1e-05)
    m1 = cols[:, 2:3] / width
    m2 = rstd * (cols[:, 3:4] - mean * cols[:, 2:3]) / width

    z_all = jnp.concatenate(
        [(outv[h] - mean) * rstd * act[h][:, 0:64] for h in range(heads)], axis=1
    )
    wo_grad = dot3(halves(z_all), gs, TN)
    if fuse:
        buf[0, 0:half] = wo_grad[:, 0:BLOCK]
        buf[0, half : 2 * half] = wo_grad[:, BLOCK : 2 * BLOCK]
        stage(0, 0)
        wopart_ref[...] = jnp.zeros(wopart_ref.shape, F32)
    else:
        wopart_ref[...] = wo_grad

    def backward(h, carry):
        val = act[h]
        u, v = val[:, 0:64], val[:, 64:128]
        q, k = val[:, 128:192], val[:, 192:256]
        nrm = (outv[h] - mean) * rstd
        dz = dzs[h]
        dn = dz * u
        du = dz * nrm
        do = halves(rstd * (dn - m1 - nrm * m2))
        da = dot3(do, halves(v), NT)
        dv = dot3(halves(attn[h]), do, TN)
        ds = halves(da * dsfac[h])
        dq = dot3(ds, halves(k), NN)
        dk = dot3(ds, halves(q), TN)
        dpre = halves(jnp.concatenate([du, dv, dq, dk], axis=1) * dsilu[h])
        buf[h + off] = dot3((xt_hi[...], xt_lo[...]), dpre, NN)
        stage(0, h + off)
        rowsum = dot(hits, dpre[0], NN) + dot(hits, dpre[1], NN)
        ws = halves(w_ref[:, pl.ds(pl.multiple_of(h * BLOCK, BLOCK), BLOCK)])
        sl[...] += dot3(halves(rowsum), ws, NT)
        for s in range(1, min(6, heads - 1 + off) + 1):
            if off == 1 and s == 1:
                stage(s, h)
            else:
                pl.when(h + off - s >= 0)(functools.partial(stage, s, h + off - s))
        return carry

    lax.fori_loop(0, heads, backward, 0)

    s_half, s_q = rows // 2, rows // 4
    s_mine = span(c * s_half + x * s_q, s_q)

    def sl_core():
        return remote(sl.at[span((1 - c) * s_half, s_half)], slc, ls.at[0], lr.at[0], at_core)

    def sl_x():
        return remote(sl.at[span(c * s_half + (1 - x) * s_q, s_q)], slx, ls.at[1], lr.at[1], at_x)

    def sl_z(k):
        return remote(sl.at[s_mine], slz.at[k], lzs.at[k], lzr.at[k], at_z[k])

    def sl_mp(k):
        return remote(slq, slm.at[k], ms.at[1, k], mr.at[1, k], at_mp[k])

    def slab(t):
        if t == 0:
            sl_core().start()
        elif t == 1:
            sl_core().wait()
            sl[span(c * s_half, s_half)] += slc[...]
            sl_x().start()
        elif t == 2:
            sl_x().wait()
            sl[s_mine] += slx[...]
            for k in range(n_z - 1):
                sl_z(k).start()
        elif t == 3:
            part = sl[s_mine]
            for k in range(n_z - 1):
                sl_z(k).wait()
                part = part + slz[k]
            slq[...] = part
            for k in range(n_mp - 1):
                sl_mp(k).start()
        elif t == 4:
            part = slq[pl.ds((z * n_mp + mp) * own, own), :]
            for k in range(n_mp - 1):
                sl_mp(k).wait()
                part = part + slm[k, pl.ds((z * n_mp + mp) * own, own), :]
            newa = accum_ref[...] + jnp.sum(part * part, axis=1, keepdims=True) / width
            newa_ref[...] = newa
            newt_ref[...] = table_ref[...] - 0.5 * part * lax.rsqrt(newa)

    slab(0)
    for t in range(1, 7):
        tick = heads - 1 + off + t
        for s in range(0, 7):
            if 0 <= tick - s < pieces:
                stage(s, tick - s)
        slab(t)


def body(layer_input, grad_out, segment, item_ids, w_uvqk, w_out, table, accum):
    count, width = layer_input.shape
    cols = w_uvqk.shape[1]
    heads = cols // BLOCK
    feats = heads * HEAD_DIM
    n_dp, n_mp = lax.axis_size("dp"), lax.axis_size("mp")
    own = table.shape[0]
    rows = own * n_dp * n_mp
    n_z = n_dp // 4
    fuse = feats * width == width * BLOCK
    pieces = heads + (1 if fuse else 0)
    half, quarter = width // 2, width // 4
    chunk = quarter // n_z
    wo_shape = (8, 128) if fuse else (feats, width)
    vmem = pl.BlockSpec(memory_space=pltpu.VMEM)
    dma = pltpu.SemaphoreType.DMA
    out, wo_part, new_table, new_accum = pl.pallas_call(
        functools.partial(kernel, n_z, n_mp, fuse),
        out_shape=(
            jax.ShapeDtypeStruct((pieces, width, BLOCK), F32),
            jax.ShapeDtypeStruct(wo_shape, F32),
            jax.ShapeDtypeStruct((own, width), F32),
            jax.ShapeDtypeStruct((own, 1), F32),
        ),
        in_specs=[vmem] * 8,
        out_specs=(vmem,) * 4,
        scratch_shapes=[
            pltpu.VMEM((pieces, width, BLOCK), F32),
            pltpu.VMEM((width, count), BF16),
            pltpu.VMEM((width, count), BF16),
            pltpu.VMEM((heads, count, BLOCK), F32),
            pltpu.VMEM((heads, count, BLOCK), F32),
            pltpu.VMEM((heads, count, count), F32),
            pltpu.VMEM((heads, count, count), F32),
            pltpu.VMEM((heads, count, HEAD_DIM), F32),
            pltpu.VMEM((heads, count, HEAD_DIM), F32),
            pltpu.VMEM((8, count), F32),
            pltpu.VMEM((n_mp - 1, 8, count), F32),
            pltpu.VMEM((pieces, half, BLOCK), F32),
            pltpu.VMEM((pieces, quarter, BLOCK), F32),
            pltpu.VMEM((pieces, n_z - 1, chunk, BLOCK), F32),
            pltpu.VMEM((rows, width), F32),
            pltpu.VMEM((rows // 2, width), F32),
            pltpu.VMEM((rows // 4, width), F32),
            pltpu.VMEM((n_z - 1, rows // 4, width), F32),
            pltpu.VMEM((rows // 4, width), F32),
            pltpu.VMEM((n_mp - 1, rows // 4, width), F32),
            dma((4, pieces)),
            dma((4, pieces)),
            dma((2, pieces, n_z - 1)),
            dma((2, pieces, n_z - 1)),
            dma((2,)),
            dma((2,)),
            dma((n_z - 1,)),
            dma((n_z - 1,)),
            dma((2, n_mp - 1)),
            dma((2, n_mp - 1)),
        ],
        compiler_params=pltpu.CompilerParams(
            collective_id=0, has_side_effects=True, vmem_limit_bytes=40 * 1024 * 1024
        ),
    )(
        layer_input,
        grad_out,
        segment,
        item_ids.reshape(1, count),
        w_uvqk,
        w_out,
        table,
        accum.reshape(own, 1),
    )
    w_uvqk_grad = jnp.concatenate([out[p] for p in range(pieces - heads, pieces)], axis=1)
    if fuse:
        w_out_grad = jnp.concatenate([out[0, :feats], out[0, feats:]], axis=1)
    else:
        w_out_grad = lax.psum(wo_part, "dp")
    return w_uvqk_grad, w_out_grad, new_table, new_accum.reshape(own)


def solution(mesh):
    placed = (
        P("dp", None),
        P("dp", None),
        P("dp", None),
        P("dp"),
        P(None, "mp"),
        P("mp", None),
        P(("dp", "mp"), None),
        P(("dp", "mp")),
    )
    return jax.shard_map(
        body,
        mesh=mesh,
        in_specs=placed,
        out_specs=(P(None, "mp"), P("mp", None), P(("dp", "mp"), None), P(("dp", "mp"))),
        check_vma=False,
    )
```

```python
import functools

import jax
import jax.numpy as jnp
from jax import lax
from jax.experimental import pallas as pl
from jax.experimental.pallas import tpu as pltpu
from jax.sharding import PartitionSpec as P

HEAD_DIM = 64
BLOCK = 4 * HEAD_DIM
MESH = pl.DeviceIdType.MESH
F32, BF16 = jnp.float32, jnp.bfloat16

NN = (((1,), (0,)), ((), ()))
NT = (((1,), (1,)), ((), ()))
TN = (((0,), (0,)), ((), ()))


def halves(value):
    high = value.astype(BF16)
    return high, (value - high.astype(F32)).astype(BF16)


def dot(left, right, dims):
    return lax.dot_general(left, right, dims, preferred_element_type=F32)


def dot3(left, right, dims):
    return dot(left[0], right[1], dims) + dot(left[1], right[0], dims) + dot(left[0], right[0], dims)


def kernel(
    n_bits, n_z, n_mp, fuse, split,
    x_hbm, g_hbm, seg_hbm, ids_hbm, w_hbm, wo_hbm, table_hbm, accum_ref,
    out, wopart_ref, newt_ref, newa_ref,
    x_ref, g_ref, seg_ref, ids_ref, w_ref, wo_ref, table_ref, in_sem,
    buf, xt_hi, xt_lo, act, dsilu, attn, dsfac, outv, dzs, stat, stat_in,
    sl, slc, slx, slz, slq, slm,
    ps, pr, ls, lr, lzs, lzr, ms, mr,
    *rcv,
):
    loads = []
    for i, (src, dst) in enumerate((
        (seg_hbm, seg_ref), (x_hbm, x_ref), (w_hbm, w_ref), (g_hbm, g_ref),
        (wo_hbm, wo_ref), (ids_hbm, ids_ref), (table_hbm, table_ref),
    )):
        loads.append(pltpu.make_async_copy(src, dst, in_sem.at[i]))
        loads[-1].start()

    count, width = x_ref.shape
    heads = w_ref.shape[1] // BLOCK
    rows = sl.shape[0]
    own = table_ref.shape[0]
    off = 1 if fuse else 0
    pieces, size = buf.shape[0], buf.shape[1]
    scale = HEAD_DIM ** (-0.5)

    dp, mp = lax.axis_index("dp"), lax.axis_index("mp")
    z, x, c = dp // 4, (dp // 2) % 2, dp % 2
    bit = [(dp // 2**i) % 2 for i in range(n_bits)]
    flip = [dp + (1 - 2 * bit[i]) * 2**i for i in range(n_bits)]
    at_core, at_x = {"dp": flip[0]}, {"dp": flip[1]}
    at_z = [{"dp": lax.rem(z + k, n_z) * 4 + x * 2 + c} for k in range(1, n_z)]
    at_mp = [{"mp": lax.rem(mp + k, n_mp)} for k in range(1, n_mp)]

    barrier = pltpu.get_barrier_semaphore()
    partners = [at_core, at_x] + at_z + at_mp
    for partner in partners:
        pl.semaphore_signal(barrier, inc=1, device_id=partner, device_id_type=MESH)

    def remote(src, dst, send, recv, where):
        return pltpu.make_async_remote_copy(
            src_ref=src, dst_ref=dst, send_sem=send, recv_sem=recv, device_id=where, device_id_type=MESH
        )

    def span(start, length):
        return pl.ds(pl.multiple_of(start, 8), length)

    def step(p, i):
        swap = (p % 4) // 3
        bits = [bit[0], bit[1] + swap * (bit[2] - bit[1]), bit[2] + swap * (bit[1] - bit[2])] + bit[3:]
        to = [flip[0], flip[1] + swap * (flip[2] - flip[1]), flip[2] + swap * (flip[1] - flip[2])] + flip[3:]
        start = 0
        for j in range(i):
            start = start + bits[j] * (size >> (j + 1))
        return bits[i], {"dp": to[i]}, start

    def reduce_copy(p, i):
        b, where, start = step(p, i)
        length = size >> (i + 1)
        return remote(
            buf.at[p, span(start + (1 - b) * length, length)], rcv[i].at[p], ps.at[i, p], pr.at[i, p], where
        )

    def gather_copy(p, i):
        b, where, start = step(p, i)
        length = size >> (i + 1)
        at = span(start + b * length, length)
        return remote(out.at[p, at], out.at[p, at], ps.at[n_bits + i, p], pr.at[n_bits + i, p], where)

    def stage(s, p):
        if s == 0:
            reduce_copy(p, 0).start()
        elif s < n_bits:
            reduce_copy(p, s - 1).wait()
            b, _, start = step(p, s)
            length = size >> (s + 1)
            buf[p, span(start + (1 - b) * length, length)] += rcv[s - 1][p, span((1 - b) * length, length)]
            reduce_copy(p, s).start()
            buf[p, span(start + b * length, length)] += rcv[s - 1][p, span(b * length, length)]
        elif s == n_bits:
            reduce_copy(p, s - 1).wait()
            b, _, start = step(p, s - 1)
            at = span(start + b * (size >> s), size >> s)
            out[p, at] = buf[p, at] + rcv[s - 1][p]
            gather_copy(p, s - 1).start()
        else:
            i = 2 * n_bits - s
            gather_copy(p, i).wait()
            if i > 0:
                gather_copy(p, i - 1).start()

    loads[0].wait()
    seg = jnp.broadcast_to(seg_ref[...].astype(F32), (count, count))
    spot = lax.broadcasted_iota(jnp.int32, (count, count), 0)
    other = lax.broadcasted_iota(jnp.int32, (count, count), 1)
    mask = jnp.where((seg == seg.T) & (spot >= other), 1.0, 0.0)
    loads[1].wait()
    xs = halves(x_ref[...])
    loads[3].wait()
    gs = halves(g_ref[...])
    loads[2].wait()
    loads[4].wait()

    def forward(h, sums):
        ws = halves(w_ref[:, pl.ds(pl.multiple_of(h * BLOCK, BLOCK), BLOCK)])
        pre = dot3(xs, ws, NN)
        sig = jax.nn.sigmoid(pre)
        val = pre * sig
        act[h] = val
        dsilu[h] = sig * (1.0 + pre * (1.0 - sig))
        u, v = val[:, 0:64], val[:, 64:128]
        q, k = val[:, 128:192], val[:, 192:256]
        score = dot3(halves(q), halves(k), NT) * scale
        ssig = jax.nn.sigmoid(score)
        a = score * ssig * mask
        attn[h] = a
        dsfac[h] = mask * (ssig * (1.0 + score * (1.0 - ssig))) * scale
        o = dot3(halves(a), halves(v), NN)
        outv[h] = o
        wos = halves(wo_ref[pl.ds(pl.multiple_of(h * HEAD_DIM, HEAD_DIM), HEAD_DIM), :])
        dz = dot3(gs, wos, NT)
        dzs[h] = dz
        dn = dz * u
        return (sums[0] + o, sums[1] + o * o, sums[2] + dn, sums[3] + dn * o)

    zero = jnp.zeros((count, HEAD_DIM), F32)
    sums = lax.fori_loop(0, heads, forward, (zero, zero, zero, zero))
    lane = lax.broadcasted_iota(jnp.int32, (count, 128), 1)
    packed = jnp.zeros((count, 128), F32)
    for i in range(4):
        packed = jnp.where(lane == i, jnp.sum(sums[i], axis=1, keepdims=True), packed)
    stat[...] = packed.T[0:8]
    pl.semaphore_wait(barrier, len(partners))

    def stat_to(k):
        return remote(stat, stat_in.at[k], ms.at[0, k], mr.at[0, k], at_mp[k])

    for k in range(n_mp - 1):
        stat_to(k).start()
    loads[5].wait()
    loads[6].wait()
    x_t = x_ref[...].T
    xt_hi[...], xt_lo[...] = halves(x_t)
    place = lax.broadcasted_iota(jnp.int32, (rows, count), 0)
    inner = n_z * n_mp * own
    pc, px = place // (2 * inner), (place // inner) % 2
    pz, pm = (place // (n_mp * own)) % n_z, place % (n_mp * own)
    wanted = ((pz * 2 + px) * 2 + pc) * (n_mp * own) + pm
    hits = jnp.where(wanted == ids_ref[...], 1.0, 0.0).astype(BF16)
    sl[...] = (dot(hits, gs[0], NN) + dot(hits, gs[1], NN)) * (1.0 / n_mp)

    total = stat[...]
    for k in range(n_mp - 1):
        stat_to(k).wait()
        total = total + stat_in[k]
    cols = jnp.concatenate([total, jnp.zeros((120, count), F32)], axis=0).T
    mean = cols[:, 0:1] / width
    var = cols[:, 1:2] / width - mean * mean
    rstd = lax.rsqrt(var + 1e-05)
    m1 = cols[:, 2:3] / width
    m2 = rstd * (cols[:, 3:4] - mean * cols[:, 2:3]) / width

    z_all = jnp.concatenate(
        [(outv[h] - mean) * rstd * act[h][:, 0:64] for h in range(heads)], axis=1
    )
    wo_grad = dot3(halves(z_all), gs, TN)
    if fuse:
        for i in range(2):
            for j in range(split // 2):
                buf[i * (split // 2) + j] = wo_grad[j * size : (j + 1) * size, i * BLOCK : (i + 1) * BLOCK]
        for p in range(split):
            for s in range(p + 1):
                stage(s, p - s)
        wopart_ref[...] = jnp.zeros(wopart_ref.shape, F32)
    else:
        wopart_ref[...] = wo_grad

    last = split * (heads + off) - 1

    def tick(piece, low):
        stage(0, piece)
        for s in range(1, min(2 * n_bits, last) + 1):
            if s <= low:
                stage(s, piece - s)
            else:
                pl.when(piece >= s)(functools.partial(stage, s, piece - s))

    def backward(h, carry):
        val = act[h]
        u, v = val[:, 0:64], val[:, 64:128]
        q, k = val[:, 128:192], val[:, 192:256]
        nrm = (outv[h] - mean) * rstd
        dz = dzs[h]
        dn = dz * u
        du = dz * nrm
        do = halves(rstd * (dn - m1 - nrm * m2))
        da = dot3(do, halves(v), NT)
        dv = dot3(halves(attn[h]), do, TN)
        ds = halves(da * dsfac[h])
        dq = dot3(ds, halves(k), NN)
        dk = dot3(ds, halves(q), TN)
        dpre = halves(jnp.concatenate([du, dv, dq, dk], axis=1) * dsilu[h])
        for j in range(split):
            part = slice(j * size, (j + 1) * size)
            buf[(h + off) * split + j] = dot3((xt_hi[part], xt_lo[part]), dpre, NN)
            if j == split - 1:
                rowsum = dot(hits, dpre[0], NN) + dot(hits, dpre[1], NN)
                ws = halves(w_ref[:, pl.ds(pl.multiple_of(h * BLOCK, BLOCK), BLOCK)])
                sl[...] += dot3(halves(rowsum), ws, NT)
            tick((h + off) * split + j, off * split + j)
        return carry

    lax.fori_loop(0, heads, backward, 0)

    s_half, s_q = rows // 2, rows // 4
    s_mine = span(c * s_half + x * s_q, s_q)

    def sl_core():
        return remote(sl.at[span((1 - c) * s_half, s_half)], slc, ls.at[0], lr.at[0], at_core)

    def sl_x():
        return remote(sl.at[span(c * s_half + (1 - x) * s_q, s_q)], slx, ls.at[1], lr.at[1], at_x)

    def sl_z(k):
        return remote(sl.at[s_mine], slz.at[k], lzs.at[k], lzr.at[k], at_z[k])

    def sl_mp(k):
        return remote(slq, slm.at[k], ms.at[1, k], mr.at[1, k], at_mp[k])

    def slab(t):
        if t == 0:
            sl_core().start()
        elif t == 1:
            sl_core().wait()
            sl[span(c * s_half, s_half)] += slc[...]
            sl_x().start()
        elif t == 2:
            sl_x().wait()
            sl[s_mine] += slx[...]
            for k in range(n_z - 1):
                sl_z(k).start()
        elif t == 3:
            part = sl[s_mine]
            for k in range(n_z - 1):
                sl_z(k).wait()
                part = part + slz[k]
            slq[...] = part
            for k in range(n_mp - 1):
                sl_mp(k).start()
        elif t == 4:
            part = slq[pl.ds((z * n_mp + mp) * own, own), :]
            for k in range(n_mp - 1):
                sl_mp(k).wait()
                part = part + slm[k, pl.ds((z * n_mp + mp) * own, own), :]
            newa = accum_ref[...] + jnp.sum(part * part, axis=1, keepdims=True) / width
            newa_ref[...] = newa
            newt_ref[...] = table_ref[...] - 0.5 * part * lax.rsqrt(newa)

    slab(0)
    for t in range(1, 2 * n_bits + 1):
        for s in range(0, 2 * n_bits + 1):
            if 0 <= last + t - s <= last:
                stage(s, last + t - s)
        if t <= 4:
            slab(t)


def body(layer_input, grad_out, segment, item_ids, w_uvqk, w_out, table, accum):
    count, width = layer_input.shape
    cols = w_uvqk.shape[1]
    heads = cols // BLOCK
    feats = heads * HEAD_DIM
    n_dp, n_mp = lax.axis_size("dp"), lax.axis_size("mp")
    own = table.shape[0]
    rows = own * n_dp * n_mp
    n_z = n_dp // 4
    fuse = feats == BLOCK and width // 2 // n_dp >= 8
    split = 2 if fuse else 1
    pieces = split * (heads + (1 if fuse else 0))
    size = width // split
    n_bits = n_dp.bit_length() - 1
    wo_shape = (8, 128) if fuse else (feats, width)
    vmem = pl.BlockSpec(memory_space=pltpu.VMEM)
    dma = pltpu.SemaphoreType.DMA
    out, wo_part, new_table, new_accum = pl.pallas_call(
        functools.partial(kernel, n_bits, n_z, n_mp, fuse, split),
        out_shape=(
            jax.ShapeDtypeStruct((pieces, size, BLOCK), F32),
            jax.ShapeDtypeStruct(wo_shape, F32),
            jax.ShapeDtypeStruct((own, width), F32),
            jax.ShapeDtypeStruct((own, 1), F32),
        ),
        in_specs=[pl.BlockSpec(memory_space=pl.ANY)] * 7 + [vmem],
        out_specs=(vmem,) * 4,
        scratch_shapes=[
            pltpu.VMEM((count, width), F32),
            pltpu.VMEM((count, width), F32),
            pltpu.VMEM((1, count), jnp.int32),
            pltpu.VMEM((1, count), jnp.int32),
            pltpu.VMEM((width, cols), F32),
            pltpu.VMEM((feats, width), F32),
            pltpu.VMEM((own, width), F32),
            dma((7,)),
            pltpu.VMEM((pieces, size, BLOCK), F32),
            pltpu.VMEM((width, count), BF16),
            pltpu.VMEM((width, count), BF16),
            pltpu.VMEM((heads, count, BLOCK), F32),
            pltpu.VMEM((heads, count, BLOCK), F32),
            pltpu.VMEM((heads, count, count), F32),
            pltpu.VMEM((heads, count, count), F32),
            pltpu.VMEM((heads, count, HEAD_DIM), F32),
            pltpu.VMEM((heads, count, HEAD_DIM), F32),
            pltpu.VMEM((8, count), F32),
            pltpu.VMEM((n_mp - 1, 8, count), F32),
            pltpu.VMEM((rows, width), F32),
            pltpu.VMEM((rows // 2, width), F32),
            pltpu.VMEM((rows // 4, width), F32),
            pltpu.VMEM((n_z - 1, rows // 4, width), F32),
            pltpu.VMEM((rows // 4, width), F32),
            pltpu.VMEM((n_mp - 1, rows // 4, width), F32),
            dma((2 * n_bits, pieces)),
            dma((2 * n_bits, pieces)),
            dma((2,)),
            dma((2,)),
            dma((n_z - 1,)),
            dma((n_z - 1,)),
            dma((2, n_mp - 1)),
            dma((2, n_mp - 1)),
        ] + [pltpu.VMEM((pieces, size >> (i + 1), BLOCK), F32) for i in range(n_bits)],
        compiler_params=pltpu.CompilerParams(
            collective_id=0, has_side_effects=True, vmem_limit_bytes=56 * 1024 * 1024
        ),
    )(
        layer_input,
        grad_out,
        segment,
        item_ids.reshape(1, count),
        w_uvqk,
        w_out,
        table,
        accum.reshape(own, 1),
    )
    out = out.reshape(pieces // split, width, BLOCK)
    w_uvqk_grad = jnp.concatenate([out[p] for p in range(pieces // split - heads, pieces // split)], axis=1)
    if fuse:
        w_out_grad = jnp.concatenate([out[0, :feats], out[0, feats:]], axis=1)
    else:
        w_out_grad = lax.psum(wo_part, "dp")
    return w_uvqk_grad, w_out_grad, new_table, new_accum.reshape(own)


def solution(mesh):
    placed = (
        P("dp", None),
        P("dp", None),
        P("dp", None),
        P("dp"),
        P(None, "mp"),
        P("mp", None),
        P(("dp", "mp"), None),
        P(("dp", "mp")),
    )
    return jax.shard_map(
        body,
        mesh=mesh,
        in_specs=placed,
        out_specs=(P(None, "mp"), P("mp", None), P(("dp", "mp"), None), P(("dp", "mp"))),
        check_vma=False,
    )
```

```python
import functools

import jax
import jax.numpy as jnp
from jax import lax
from jax.experimental import pallas as pl
from jax.experimental.pallas import tpu as pltpu
from jax.sharding import PartitionSpec as P

HEAD_DIM = 64
BLOCK = 4 * HEAD_DIM
MESH = pl.DeviceIdType.MESH
F32, BF16 = jnp.float32, jnp.bfloat16

NN = (((1,), (0,)), ((), ()))
NT = (((1,), (1,)), ((), ()))
TN = (((0,), (0,)), ((), ()))


def halves(value):
    high = value.astype(BF16)
    return high, (value - high.astype(F32)).astype(BF16)


def dot(left, right, dims):
    return lax.dot_general(left, right, dims, preferred_element_type=F32)


def dot3(left, right, dims):
    return dot(left[0], right[1], dims) + dot(left[1], right[0], dims) + dot(left[0], right[0], dims)


def remote(src, dst, send, recv, where):
    return pltpu.make_async_remote_copy(
        src_ref=src, dst_ref=dst, send_sem=send, recv_sem=recv, device_id=where, device_id_type=MESH
    )


def span(start, length):
    return pl.ds(pl.multiple_of(start, 8), length)


def compute_kernel(
    n_z, n_mp, fuse,
    x_hbm, g_hbm, seg_hbm, ids_hbm, w_hbm, wo_hbm,
    buf, sl, wopart_ref,
    x_ref, g_ref, seg_ref, ids_ref, w_ref, wo_ref, in_sem,
    xt_hi, xt_lo, act, dsilu, attn, dsfac, outv, dzs, stat, stat_in, ms, mr,
):
    loads = []
    for i, (src, dst) in enumerate((
        (seg_hbm, seg_ref), (x_hbm, x_ref), (w_hbm, w_ref), (g_hbm, g_ref),
        (wo_hbm, wo_ref), (ids_hbm, ids_ref),
    )):
        loads.append(pltpu.make_async_copy(src, dst, in_sem.at[i]))
        loads[-1].start()
    count, width = x_ref.shape
    heads = w_ref.shape[1] // BLOCK
    rows = sl.shape[0]
    off = 1 if fuse else 0
    scale = HEAD_DIM ** (-0.5)
    mp = lax.axis_index("mp")
    at_mp = [{"mp": lax.rem(mp + k, n_mp)} for k in range(1, n_mp)]
    own = rows // (n_z * 4 * n_mp)
    barrier = pltpu.get_barrier_semaphore()
    for partner in at_mp:
        pl.semaphore_signal(barrier, inc=1, device_id=partner, device_id_type=MESH)

    loads[0].wait()
    seg = jnp.broadcast_to(seg_ref[...].astype(F32), (count, count))
    spot = lax.broadcasted_iota(jnp.int32, (count, count), 0)
    other = lax.broadcasted_iota(jnp.int32, (count, count), 1)
    mask = jnp.where((seg == seg.T) & (spot >= other), 1.0, 0.0)
    loads[1].wait()
    xs = halves(x_ref[...])
    loads[3].wait()
    gs = halves(g_ref[...])
    loads[2].wait()
    loads[4].wait()

    def forward(h, sums):
        ws = halves(w_ref[:, pl.ds(pl.multiple_of(h * BLOCK, BLOCK), BLOCK)])
        pre = dot3(xs, ws, NN)
        sig = jax.nn.sigmoid(pre)
        val = pre * sig
        act[h] = val
        dsilu[h] = sig * (1.0 + pre * (1.0 - sig))
        u, v = val[:, 0:64], val[:, 64:128]
        q, k = val[:, 128:192], val[:, 192:256]
        score = dot3(halves(q), halves(k), NT) * scale
        ssig = jax.nn.sigmoid(score)
        a = score * ssig * mask
        attn[h] = a
        dsfac[h] = mask * (ssig * (1.0 + score * (1.0 - ssig))) * scale
        o = dot3(halves(a), halves(v), NN)
        outv[h] = o
        wos = halves(wo_ref[pl.ds(pl.multiple_of(h * HEAD_DIM, HEAD_DIM), HEAD_DIM), :])
        dz = dot3(gs, wos, NT)
        dzs[h] = dz
        dn = dz * u
        return (sums[0] + o, sums[1] + o * o, sums[2] + dn, sums[3] + dn * o)

    zero = jnp.zeros((count, HEAD_DIM), F32)
    sums = lax.fori_loop(0, heads, forward, (zero, zero, zero, zero))
    lane = lax.broadcasted_iota(jnp.int32, (count, 128), 1)
    packed = jnp.zeros((count, 128), F32)
    for i in range(4):
        packed = jnp.where(lane == i, jnp.sum(sums[i], axis=1, keepdims=True), packed)
    stat[...] = packed.T[0:8]
    pl.semaphore_wait(barrier, len(at_mp))

    def stat_to(k):
        return remote(stat, stat_in.at[k], ms.at[k], mr.at[k], at_mp[k])

    for k in range(n_mp - 1):
        stat_to(k).start()
    loads[5].wait()
    x_t = x_ref[...].T
    xt_hi[...], xt_lo[...] = halves(x_t)
    place = lax.broadcasted_iota(jnp.int32, (rows, count), 0)
    inner = n_z * n_mp * own
    pc, px = place // (2 * inner), (place // inner) % 2
    pz, pm = (place // (n_mp * own)) % n_z, place % (n_mp * own)
    wanted = ((pz * 2 + px) * 2 + pc) * (n_mp * own) + pm
    hits = jnp.where(wanted == ids_ref[...], 1.0, 0.0).astype(BF16)
    sl[...] = (dot(hits, gs[0], NN) + dot(hits, gs[1], NN)) * (1.0 / n_mp)

    total = stat[...]
    for k in range(n_mp - 1):
        stat_to(k).wait()
        total = total + stat_in[k]
    cols = jnp.concatenate([total, jnp.zeros((120, count), F32)], axis=0).T
    mean = cols[:, 0:1] / width
    var = cols[:, 1:2] / width - mean * mean
    rstd = lax.rsqrt(var + 1e-05)
    m1 = cols[:, 2:3] / width
    m2 = rstd * (cols[:, 3:4] - mean * cols[:, 2:3]) / width

    z_all = jnp.concatenate(
        [(outv[h] - mean) * rstd * act[h][:, 0:64] for h in range(heads)], axis=1
    )
    wo_grad = dot3(halves(z_all), gs, TN)
    if fuse:
        buf[0, 0:count] = wo_grad[:, 0:BLOCK]
        buf[0, count : 2 * count] = wo_grad[:, BLOCK : 2 * BLOCK]
        wopart_ref[...] = jnp.zeros(wopart_ref.shape, F32)
    else:
        wopart_ref[...] = wo_grad

    def backward(h, carry):
        val = act[h]
        u, v = val[:, 0:64], val[:, 64:128]
        q, k = val[:, 128:192], val[:, 192:256]
        nrm = (outv[h] - mean) * rstd
        dz = dzs[h]
        dn = dz * u
        du = dz * nrm
        do = halves(rstd * (dn - m1 - nrm * m2))
        da = dot3(do, halves(v), NT)
        dv = dot3(halves(attn[h]), do, TN)
        ds = halves(da * dsfac[h])
        dq = dot3(ds, halves(k), NN)
        dk = dot3(ds, halves(q), TN)
        dpre = halves(jnp.concatenate([du, dv, dq, dk], axis=1) * dsilu[h])
        buf[h + off] = dot3((xt_hi[...], xt_lo[...]), dpre, NN)
        rowsum = dot(hits, dpre[0], NN) + dot(hits, dpre[1], NN)
        ws = halves(w_ref[:, pl.ds(pl.multiple_of(h * BLOCK, BLOCK), BLOCK)])
        sl[...] += dot3(halves(rowsum), ws, NT)
        return carry

    lax.fori_loop(0, heads, backward, 0)


def sum_kernel(
    n_z, n_mp,
    part, sl, table_ref, accum_ref,
    out, newt_ref, newa_ref,
    acc, rc, rx, rz, sla, slc, slx, slz, slq, slm,
    ps, pr, zs, zr, ls, lr, lzs, lzr, ms, mr,
):
    pieces, width = part.shape[0], sl.shape[1]
    half = part.shape[1] // 2
    quarter = half // 2
    chunk = quarter // n_z
    rows, own = sl.shape[0], table_ref.shape[0]
    dp, mp = lax.axis_index("dp"), lax.axis_index("mp")
    z, x, c = dp // 4, (dp // 2) % 2, dp % 2
    at_core = {"dp": z * 4 + x * 2 + (1 - c)}
    at_x = {"dp": z * 4 + (1 - x) * 2 + c}
    z_of = [lax.rem(z + k, n_z) for k in range(1, n_z)]
    at_z = [{"dp": zz * 4 + x * 2 + c} for zz in z_of]
    at_mp = [{"mp": lax.rem(mp + k, n_mp)} for k in range(1, n_mp)]
    barrier = pltpu.get_barrier_semaphore()
    partners = [at_core, at_x] + at_z + at_mp
    for partner in partners:
        pl.semaphore_signal(barrier, inc=1, device_id=partner, device_id_type=MESH)
    pl.semaphore_wait(barrier, len(partners))

    mine = span(c * half, half)
    theirs = span((1 - c) * half, half)
    my_q, their_q = span(x * quarter, quarter), span((1 - x) * quarter, quarter)
    out_q = span(c * half + x * quarter, quarter)
    my_chunk = span(c * half + x * quarter + z * chunk, chunk)

    def core_rs(p):
        return remote(part.at[p, theirs], rc.at[p], ps.at[0, p], pr.at[0, p], at_core)

    def x_rs(p):
        return remote(acc.at[p, their_q], rx.at[p], ps.at[1, p], pr.at[1, p], at_x)

    def z_rs(p, k):
        there = span(x * quarter + z_of[k] * chunk, chunk)
        return remote(acc.at[p, there], rz.at[p, k], zs.at[0, p, k], zr.at[0, p, k], at_z[k])

    def z_ag(p, k):
        return remote(out.at[p, my_chunk], out.at[p, my_chunk], zs.at[1, p, k], zr.at[1, p, k], at_z[k])

    def x_ag(p):
        return remote(out.at[p, out_q], out.at[p, out_q], ps.at[2, p], pr.at[2, p], at_x)

    def core_ag(p):
        return remote(out.at[p, mine], out.at[p, mine], ps.at[3, p], pr.at[3, p], at_core)

    def stage(s, p):
        if s == 0:
            core_rs(p).start()
        elif s == 1:
            core_rs(p).wait()
            acc[p, their_q] = part[p, span(c * half + (1 - x) * quarter, quarter)] + rc[p, their_q]
            x_rs(p).start()
            acc[p, my_q] = part[p, out_q] + rc[p, my_q]
        elif s == 2:
            x_rs(p).wait()
            acc[p, my_q] += rx[p]
            for k in range(n_z - 1):
                z_rs(p, k).start()
        elif s == 3:
            total = acc[p, span(x * quarter + z * chunk, chunk)]
            for k in range(n_z - 1):
                z_rs(p, k).wait()
                total = total + rz[p, k]
            out[p, my_chunk] = total
            for k in range(n_z - 1):
                z_ag(p, k).start()
        elif s == 4:
            for k in range(n_z - 1):
                z_ag(p, k).wait()
            x_ag(p).start()
        elif s == 5:
            x_ag(p).wait()
            core_ag(p).start()
        else:
            core_ag(p).wait()

    s_half, s_q = rows // 2, rows // 4
    s_mine, s_theirs = span(x * s_q, s_q), span((1 - x) * s_q, s_q)

    def sl_core():
        return remote(sl.at[span((1 - c) * s_half, s_half)], slc, ls.at[0], lr.at[0], at_core)

    def sl_x():
        return remote(sla.at[s_theirs], slx, ls.at[1], lr.at[1], at_x)

    def sl_z(k):
        return remote(sla.at[s_mine], slz.at[k], lzs.at[k], lzr.at[k], at_z[k])

    def sl_mp(k):
        return remote(slq, slm.at[k], ms.at[k], mr.at[k], at_mp[k])

    def slab(t):
        if t == 0:
            sl_core().start()
        elif t == 1:
            sl_core().wait()
            sla[...] = sl[span(c * s_half, s_half)] + slc[...]
            sl_x().start()
        elif t == 2:
            sl_x().wait()
            sla[s_mine] += slx[...]
            for k in range(n_z - 1):
                sl_z(k).start()
        elif t == 3:
            row = sla[s_mine]
            for k in range(n_z - 1):
                sl_z(k).wait()
                row = row + slz[k]
            slq[...] = row
            for k in range(n_mp - 1):
                sl_mp(k).start()
        elif t == 4:
            row = slq[pl.ds((z * n_mp + mp) * own, own), :]
            for k in range(n_mp - 1):
                sl_mp(k).wait()
                row = row + slm[k, pl.ds((z * n_mp + mp) * own, own), :]
            newa = accum_ref[...] + jnp.sum(row * row, axis=1, keepdims=True) / width
            newa_ref[...] = newa
            newt_ref[...] = table_ref[...] - 0.5 * row * lax.rsqrt(newa)

    for s in range(7):
        for p in range(pieces):
            stage(s, p)
        if s <= 4:
            slab(s)


def body(layer_input, grad_out, segment, item_ids, w_uvqk, w_out, table, accum):
    count, width = layer_input.shape
    cols = w_uvqk.shape[1]
    heads = cols // BLOCK
    feats = heads * HEAD_DIM
    n_dp, n_mp = lax.axis_size("dp"), lax.axis_size("mp")
    own = table.shape[0]
    rows = own * n_dp * n_mp
    n_z = n_dp // 4
    fuse = feats == BLOCK and width // 2 // n_dp >= 8
    pieces = heads + (1 if fuse else 0)
    half, quarter = width // 2, width // 4
    chunk = quarter // n_z
    wo_shape = (8, 128) if fuse else (feats, width)
    vmem = pl.BlockSpec(memory_space=pltpu.VMEM)
    hbm = pl.BlockSpec(memory_space=pl.ANY)
    dma = pltpu.SemaphoreType.DMA
    parts, slab, wo_part = pl.pallas_call(
        functools.partial(compute_kernel, n_z, n_mp, fuse),
        out_shape=(
            jax.ShapeDtypeStruct((pieces, width, BLOCK), F32),
            jax.ShapeDtypeStruct((rows, width), F32),
            jax.ShapeDtypeStruct(wo_shape, F32),
        ),
        in_specs=[hbm] * 6,
        out_specs=(vmem,) * 3,
        scratch_shapes=[
            pltpu.VMEM((count, width), F32),
            pltpu.VMEM((count, width), F32),
            pltpu.VMEM((1, count), jnp.int32),
            pltpu.VMEM((1, count), jnp.int32),
            pltpu.VMEM((width, cols), F32),
            pltpu.VMEM((feats, width), F32),
            dma((6,)),
            pltpu.VMEM((width, count), BF16),
            pltpu.VMEM((width, count), BF16),
            pltpu.VMEM((heads, count, BLOCK), F32),
            pltpu.VMEM((heads, count, BLOCK), F32),
            pltpu.VMEM((heads, count, count), F32),
            pltpu.VMEM((heads, count, count), F32),
            pltpu.VMEM((heads, count, HEAD_DIM), F32),
            pltpu.VMEM((heads, count, HEAD_DIM), F32),
            pltpu.VMEM((8, count), F32),
            pltpu.VMEM((n_mp - 1, 8, count), F32),
            dma((n_mp - 1,)),
            dma((n_mp - 1,)),
        ],
        compiler_params=pltpu.CompilerParams(
            collective_id=0, has_side_effects=True, vmem_limit_bytes=56 * 1024 * 1024
        ),
    )(layer_input, grad_out, segment, item_ids.reshape(1, count), w_uvqk, w_out)
    out, new_table, new_accum = pl.pallas_call(
        functools.partial(sum_kernel, n_z, n_mp),
        out_shape=(
            jax.ShapeDtypeStruct((pieces, width, BLOCK), F32),
            jax.ShapeDtypeStruct((own, width), F32),
            jax.ShapeDtypeStruct((own, 1), F32),
        ),
        in_specs=[vmem] * 4,
        out_specs=(vmem,) * 3,
        scratch_shapes=[
            pltpu.VMEM((pieces, half, BLOCK), F32),
            pltpu.VMEM((pieces, half, BLOCK), F32),
            pltpu.VMEM((pieces, quarter, BLOCK), F32),
            pltpu.VMEM((pieces, n_z - 1, chunk, BLOCK), F32),
            pltpu.VMEM((rows // 2, width), F32),
            pltpu.VMEM((rows // 2, width), F32),
            pltpu.VMEM((rows // 4, width), F32),
            pltpu.VMEM((n_z - 1, rows // 4, width), F32),
            pltpu.VMEM((rows // 4, width), F32),
            pltpu.VMEM((n_mp - 1, rows // 4, width), F32),
            dma((4, pieces)),
            dma((4, pieces)),
            dma((2, pieces, n_z - 1)),
            dma((2, pieces, n_z - 1)),
            dma((2,)),
            dma((2,)),
            dma((n_z - 1,)),
            dma((n_z - 1,)),
            dma((n_mp - 1,)),
            dma((n_mp - 1,)),
        ],
        compiler_params=pltpu.CompilerParams(
            collective_id=1, has_side_effects=True, vmem_limit_bytes=30 * 1024 * 1024
        ),
    )(parts, slab, table, accum.reshape(own, 1))
    w_uvqk_grad = jnp.concatenate([out[p] for p in range(pieces - heads, pieces)], axis=1)
    if fuse:
        w_out_grad = jnp.concatenate([out[0, :feats], out[0, feats:]], axis=1)
    else:
        w_out_grad = lax.psum(wo_part, "dp")
    return w_uvqk_grad, w_out_grad, new_table, new_accum.reshape(own)


def solution(mesh):
    placed = (
        P("dp", None),
        P("dp", None),
        P("dp", None),
        P("dp"),
        P(None, "mp"),
        P("mp", None),
        P(("dp", "mp"), None),
        P(("dp", "mp")),
    )
    return jax.shard_map(
        body,
        mesh=mesh,
        in_specs=placed,
        out_specs=(P(None, "mp"), P("mp", None), P(("dp", "mp"), None), P(("dp", "mp"))),
        check_vma=False,
    )
```

```python
import functools

import jax
import jax.numpy as jnp
from jax import lax
from jax.experimental import pallas as pl
from jax.experimental.pallas import tpu as pltpu
from jax.sharding import PartitionSpec as P

HEAD_DIM = 64
BLOCK = 4 * HEAD_DIM
MESH = pl.DeviceIdType.MESH
F32, BF16 = jnp.float32, jnp.bfloat16

NN = (((1,), (0,)), ((), ()))
NT = (((1,), (1,)), ((), ()))
TN = (((0,), (0,)), ((), ()))


def halves(value):
    high = value.astype(BF16)
    return high, (value - high.astype(F32)).astype(BF16)


def dot(left, right, dims):
    return lax.dot_general(left, right, dims, preferred_element_type=F32)


def dot3(left, right, dims):
    return dot(left[0], right[1], dims) + dot(left[1], right[0], dims) + dot(left[0], right[0], dims)


def kernel(
    n_z, n_mp, fuse,
    x_hbm, g_hbm, seg_hbm, ids_hbm, w_hbm, wo_hbm, table_hbm, accum_ref,
    out_hbm, wopart_ref, newt_ref, newa_ref,
    x_ref, g_ref, seg_ref, ids_ref, w_ref, wo_ref, table_ref, in_sem, out_sem,
    out, buf, xt_hi, xt_lo, act, dsilu, attn, dsfac, outv, dzs, stat, stat_in,
    rc, rx, rz, sl, slc, slx, slz, slq, slm,
    ps, pr, zs, zr, ls, lr, lzs, lzr, ms, mr,
):
    loads = []
    for i, (src, dst) in enumerate((
        (seg_hbm, seg_ref), (x_hbm, x_ref), (w_hbm, w_ref), (g_hbm, g_ref),
        (wo_hbm, wo_ref), (ids_hbm, ids_ref), (table_hbm, table_ref),
    )):
        loads.append(pltpu.make_async_copy(src, dst, in_sem.at[i]))
        loads[-1].start()
    count, width = x_ref.shape
    heads = w_ref.shape[1] // BLOCK
    rows = sl.shape[0]
    own = table_ref.shape[0]
    off = 1 if fuse else 0
    pieces = heads + off
    half = buf.shape[1] // 2
    quarter = half // 2
    chunk = quarter // n_z
    scale = HEAD_DIM ** (-0.5)

    dp, mp = lax.axis_index("dp"), lax.axis_index("mp")
    z, x, c = dp // 4, (dp // 2) % 2, dp % 2
    at_core = {"dp": z * 4 + x * 2 + (1 - c)}
    at_x = {"dp": z * 4 + (1 - x) * 2 + c}
    z_of = [lax.rem(z + k, n_z) for k in range(1, n_z)]
    at_z = [{"dp": zz * 4 + x * 2 + c} for zz in z_of]
    at_mp = [{"mp": lax.rem(mp + k, n_mp)} for k in range(1, n_mp)]

    barrier = pltpu.get_barrier_semaphore()
    partners = [at_core, at_x] + at_z + at_mp
    for partner in partners:
        pl.semaphore_signal(barrier, inc=1, device_id=partner, device_id_type=MESH)

    def remote(src, dst, send, recv, where):
        return pltpu.make_async_remote_copy(
            src_ref=src, dst_ref=dst, send_sem=send, recv_sem=recv, device_id=where, device_id_type=MESH
        )

    def span(start, size):
        return pl.ds(pl.multiple_of(start, 8), size)

    mine = span(c * half, half)
    theirs = span((1 - c) * half, half)
    my_q = span(c * half + x * quarter, quarter)
    their_q = span(c * half + (1 - x) * quarter, quarter)
    my_chunk = span(c * half + x * quarter + z * chunk, chunk)

    def core_rs(p):
        return remote(buf.at[p, theirs], rc.at[p], ps.at[0, p], pr.at[0, p], at_core)

    def x_rs(p):
        return remote(buf.at[p, their_q], rx.at[p], ps.at[1, p], pr.at[1, p], at_x)

    def z_rs(p, k):
        part = span(c * half + x * quarter + z_of[k] * chunk, chunk)
        return remote(buf.at[p, part], rz.at[p, k], zs.at[0, p, k], zr.at[0, p, k], at_z[k])

    def z_ag(p, k):
        return remote(out.at[p, my_chunk], out.at[p, my_chunk], zs.at[1, p, k], zr.at[1, p, k], at_z[k])

    def x_ag(p):
        return remote(out.at[p, my_q], out.at[p, my_q], ps.at[2, p], pr.at[2, p], at_x)

    def core_ag(p):
        return remote(out.at[p, mine], out.at[p, mine], ps.at[3, p], pr.at[3, p], at_core)

    def keep(p):
        return pltpu.make_async_copy(out.at[p], out_hbm.at[p], out_sem.at[p])

    def stage(s, p):
        if s == 0:
            core_rs(p).start()
        elif s == 1:
            core_rs(p).wait()
            buf[p, their_q] += rc[p, span((1 - x) * quarter, quarter)]
            x_rs(p).start()
            buf[p, my_q] += rc[p, span(x * quarter, quarter)]
        elif s == 2:
            x_rs(p).wait()
            buf[p, my_q] += rx[p]
            for k in range(n_z - 1):
                z_rs(p, k).start()
        elif s == 3:
            total = buf[p, my_chunk]
            for k in range(n_z - 1):
                z_rs(p, k).wait()
                total = total + rz[p, k]
            out[p, my_chunk] = total
            for k in range(n_z - 1):
                z_ag(p, k).start()
        elif s == 4:
            for k in range(n_z - 1):
                z_ag(p, k).wait()
            x_ag(p).start()
        elif s == 5:
            x_ag(p).wait()
            core_ag(p).start()
        else:
            core_ag(p).wait()
            keep(p).start()

    loads[0].wait()
    seg = jnp.broadcast_to(seg_ref[...].astype(F32), (count, count))
    spot = lax.broadcasted_iota(jnp.int32, (count, count), 0)
    other = lax.broadcasted_iota(jnp.int32, (count, count), 1)
    mask = jnp.where((seg == seg.T) & (spot >= other), 1.0, 0.0)
    loads[1].wait()
    xs = halves(x_ref[...])
    loads[3].wait()
    gs = halves(g_ref[...])
    loads[2].wait()
    loads[4].wait()

    def forward(h, sums):
        ws = halves(w_ref[:, pl.ds(pl.multiple_of(h * BLOCK, BLOCK), BLOCK)])
        pre = dot3(xs, ws, NN)
        sig = jax.nn.sigmoid(pre)
        val = pre * sig
        act[h] = val
        dsilu[h] = sig * (1.0 + pre * (1.0 - sig))
        u, v = val[:, 0:64], val[:, 64:128]
        q, k = val[:, 128:192], val[:, 192:256]
        score = dot3(halves(q), halves(k), NT) * scale
        ssig = jax.nn.sigmoid(score)
        a = score * ssig * mask
        attn[h] = a
        dsfac[h] = mask * (ssig * (1.0 + score * (1.0 - ssig))) * scale
        o = dot3(halves(a), halves(v), NN)
        outv[h] = o
        wos = halves(wo_ref[pl.ds(pl.multiple_of(h * HEAD_DIM, HEAD_DIM), HEAD_DIM), :])
        dz = dot3(gs, wos, NT)
        dzs[h] = dz
        dn = dz * u
        return (sums[0] + o, sums[1] + o * o, sums[2] + dn, sums[3] + dn * o)

    zero = jnp.zeros((count, HEAD_DIM), F32)
    sums = lax.fori_loop(0, heads, forward, (zero, zero, zero, zero))
    lane = lax.broadcasted_iota(jnp.int32, (count, 128), 1)
    packed = jnp.zeros((count, 128), F32)
    for i in range(4):
        packed = jnp.where(lane == i, jnp.sum(sums[i], axis=1, keepdims=True), packed)
    stat[...] = packed.T[0:8]
    pl.semaphore_wait(barrier, len(partners))

    def stat_to(k):
        return remote(stat, stat_in.at[k], ms.at[0, k], mr.at[0, k], at_mp[k])

    for k in range(n_mp - 1):
        stat_to(k).start()
    loads[5].wait()
    loads[6].wait()
    x_t = x_ref[...].T
    xt_hi[...], xt_lo[...] = halves(x_t)
    place = lax.broadcasted_iota(jnp.int32, (rows, count), 0)
    inner = n_z * n_mp * own
    pc, px = place // (2 * inner), (place // inner) % 2
    pz, pm = (place // (n_mp * own)) % n_z, place % (n_mp * own)
    wanted = ((pz * 2 + px) * 2 + pc) * (n_mp * own) + pm
    hits = jnp.where(wanted == ids_ref[...], 1.0, 0.0).astype(BF16)
    sl[...] = (dot(hits, gs[0], NN) + dot(hits, gs[1], NN)) * (1.0 / n_mp)

    total = stat[...]
    for k in range(n_mp - 1):
        stat_to(k).wait()
        total = total + stat_in[k]
    cols = jnp.concatenate([total, jnp.zeros((120, count), F32)], axis=0).T
    mean = cols[:, 0:1] / width
    var = cols[:, 1:2] / width - mean * mean
    rstd = lax.rsqrt(var + 1e-05)
    m1 = cols[:, 2:3] / width
    m2 = rstd * (cols[:, 3:4] - mean * cols[:, 2:3]) / width

    z_all = jnp.concatenate(
        [(outv[h] - mean) * rstd * act[h][:, 0:64] for h in range(heads)], axis=1
    )
    wo_grad = dot3(halves(z_all), gs, TN)
    if fuse:
        buf[0, 0:half] = wo_grad[:, 0:BLOCK]
        buf[0, half : 2 * half] = wo_grad[:, BLOCK : 2 * BLOCK]
        stage(0, 0)
        wopart_ref[...] = jnp.zeros(wopart_ref.shape, F32)
    else:
        wopart_ref[...] = wo_grad

    def backward(h, carry):
        val = act[h]
        u, v = val[:, 0:64], val[:, 64:128]
        q, k = val[:, 128:192], val[:, 192:256]
        nrm = (outv[h] - mean) * rstd
        dz = dzs[h]
        dn = dz * u
        du = dz * nrm
        do = halves(rstd * (dn - m1 - nrm * m2))
        da = dot3(do, halves(v), NT)
        dv = dot3(halves(attn[h]), do, TN)
        ds = halves(da * dsfac[h])
        dq = dot3(ds, halves(k), NN)
        dk = dot3(ds, halves(q), TN)
        dpre = halves(jnp.concatenate([du, dv, dq, dk], axis=1) * dsilu[h])
        buf[h + off] = dot3((xt_hi[...], xt_lo[...]), dpre, NN)
        stage(0, h + off)
        rowsum = dot(hits, dpre[0], NN) + dot(hits, dpre[1], NN)
        ws = halves(w_ref[:, pl.ds(pl.multiple_of(h * BLOCK, BLOCK), BLOCK)])
        sl[...] += dot3(halves(rowsum), ws, NT)
        for s in range(1, min(6, heads - 1 + off) + 1):
            if off == 1 and s == 1:
                stage(s, h)
            else:
                pl.when(h + off - s >= 0)(functools.partial(stage, s, h + off - s))
        return carry

    lax.fori_loop(0, heads, backward, 0)

    s_half, s_q = rows // 2, rows // 4
    s_mine = span(c * s_half + x * s_q, s_q)

    def sl_core():
        return remote(sl.at[span((1 - c) * s_half, s_half)], slc, ls.at[0], lr.at[0], at_core)

    def sl_x():
        return remote(sl.at[span(c * s_half + (1 - x) * s_q, s_q)], slx, ls.at[1], lr.at[1], at_x)

    def sl_z(k):
        return remote(sl.at[s_mine], slz.at[k], lzs.at[k], lzr.at[k], at_z[k])

    def sl_mp(k):
        return remote(slq, slm.at[k], ms.at[1, k], mr.at[1, k], at_mp[k])

    def slab(t):
        if t == 0:
            sl_core().start()
        elif t == 1:
            sl_core().wait()
            sl[span(c * s_half, s_half)] += slc[...]
            sl_x().start()
        elif t == 2:
            sl_x().wait()
            sl[s_mine] += slx[...]
            for k in range(n_z - 1):
                sl_z(k).start()
        elif t == 3:
            part = sl[s_mine]
            for k in range(n_z - 1):
                sl_z(k).wait()
                part = part + slz[k]
            slq[...] = part
            for k in range(n_mp - 1):
                sl_mp(k).start()
        elif t == 4:
            part = slq[pl.ds((z * n_mp + mp) * own, own), :]
            for k in range(n_mp - 1):
                sl_mp(k).wait()
                part = part + slm[k, pl.ds((z * n_mp + mp) * own, own), :]
            newa = accum_ref[...] + jnp.sum(part * part, axis=1, keepdims=True) / width
            newa_ref[...] = newa
            newt_ref[...] = table_ref[...] - 0.5 * part * lax.rsqrt(newa)

    slab(0)
    for t in range(1, 7):
        tick = heads - 1 + off + t
        for s in range(0, 7):
            if 0 <= tick - s < pieces:
                stage(s, tick - s)
        slab(t)
    for p in range(pieces):
        keep(p).wait()


def layout_kernel(off, pieces_ref, table_ref, *refs):
    sem = refs[-1]
    w_ref, newt_ref = refs[0], refs[1]
    moves = [(table_ref, newt_ref)]
    for h in range(w_ref.shape[1] // BLOCK):
        moves.append((pieces_ref.at[h + off], w_ref.at[:, pl.ds(h * BLOCK, BLOCK)]))
    if off:
        wo_ref = refs[2]
        count = wo_ref.shape[0]
        for i in range(2):
            moves.append((pieces_ref.at[0, pl.ds(i * count, count)], wo_ref.at[:, pl.ds(i * BLOCK, BLOCK)]))
    copies = [pltpu.make_async_copy(src, dst, sem.at[i]) for i, (src, dst) in enumerate(moves)]
    for copy in copies:
        copy.start()
    for copy in copies:
        copy.wait()


def body(layer_input, grad_out, segment, item_ids, w_uvqk, w_out, table, accum):
    count, width = layer_input.shape
    cols = w_uvqk.shape[1]
    heads = cols // BLOCK
    feats = heads * HEAD_DIM
    n_dp, n_mp = lax.axis_size("dp"), lax.axis_size("mp")
    own = table.shape[0]
    rows = own * n_dp * n_mp
    n_z = n_dp // 4
    fuse = feats == BLOCK
    pieces = heads + (1 if fuse else 0)
    half, quarter = width // 2, width // 4
    chunk = quarter // n_z
    wo_shape = (8, 128) if fuse else (feats, width)
    vmem = pl.BlockSpec(memory_space=pltpu.VMEM)
    hbm = pl.BlockSpec(memory_space=pl.ANY)
    dma = pltpu.SemaphoreType.DMA
    out, wo_part, new_table, new_accum = pl.pallas_call(
        functools.partial(kernel, n_z, n_mp, fuse),
        out_shape=(
            jax.ShapeDtypeStruct((pieces, width, BLOCK), F32),
            jax.ShapeDtypeStruct(wo_shape, F32),
            jax.ShapeDtypeStruct((own, width), F32),
            jax.ShapeDtypeStruct((own, 1), F32),
        ),
        in_specs=[hbm] * 7 + [vmem],
        out_specs=(hbm, vmem, vmem, vmem),
        scratch_shapes=[
            pltpu.VMEM((count, width), F32),
            pltpu.VMEM((count, width), F32),
            pltpu.VMEM((1, count), jnp.int32),
            pltpu.VMEM((1, count), jnp.int32),
            pltpu.VMEM((width, cols), F32),
            pltpu.VMEM((feats, width), F32),
            pltpu.VMEM((own, width), F32),
            dma((7,)),
            dma((pieces,)),
            pltpu.VMEM((pieces, width, BLOCK), F32),
            pltpu.VMEM((pieces, width, BLOCK), F32),
            pltpu.VMEM((width, count), BF16),
            pltpu.VMEM((width, count), BF16),
            pltpu.VMEM((heads, count, BLOCK), F32),
            pltpu.VMEM((heads, count, BLOCK), F32),
            pltpu.VMEM((heads, count, count), F32),
            pltpu.VMEM((heads, count, count), F32),
            pltpu.VMEM((heads, count, HEAD_DIM), F32),
            pltpu.VMEM((heads, count, HEAD_DIM), F32),
            pltpu.VMEM((8, count), F32),
            pltpu.VMEM((n_mp - 1, 8, count), F32),
            pltpu.VMEM((pieces, half, BLOCK), F32),
            pltpu.VMEM((pieces, quarter, BLOCK), F32),
            pltpu.VMEM((pieces, n_z - 1, chunk, BLOCK), F32),
            pltpu.VMEM((rows, width), F32),
            pltpu.VMEM((rows // 2, width), F32),
            pltpu.VMEM((rows // 4, width), F32),
            pltpu.VMEM((n_z - 1, rows // 4, width), F32),
            pltpu.VMEM((rows // 4, width), F32),
            pltpu.VMEM((n_mp - 1, rows // 4, width), F32),
            dma((4, pieces)),
            dma((4, pieces)),
            dma((2, pieces, n_z - 1)),
            dma((2, pieces, n_z - 1)),
            dma((2,)),
            dma((2,)),
            dma((n_z - 1,)),
            dma((n_z - 1,)),
            dma((2, n_mp - 1)),
            dma((2, n_mp - 1)),
        ],
        compiler_params=pltpu.CompilerParams(
            collective_id=0, has_side_effects=True, vmem_limit_bytes=56 * 1024 * 1024
        ),
    )(
        layer_input,
        grad_out,
        segment,
        item_ids.reshape(1, count),
        w_uvqk,
        w_out,
        table,
        accum.reshape(own, 1),
    )
    results = [
        jax.ShapeDtypeStruct((width, cols), F32),
        jax.ShapeDtypeStruct((own, width), F32),
    ] + ([jax.ShapeDtypeStruct((feats, width), F32)] if fuse else [])
    laid = pl.pallas_call(
        functools.partial(layout_kernel, 1 if fuse else 0),
        out_shape=tuple(results),
        in_specs=[hbm] * 2,
        out_specs=(hbm,) * len(results),
        scratch_shapes=[dma((heads + 3,))],
        compiler_params=pltpu.CompilerParams(vmem_limit_bytes=56 * 1024 * 1024),
    )(out, new_table)
    w_uvqk_grad, new_table = laid[:2]
    w_out_grad = laid[2] if fuse else lax.psum(wo_part, "dp")
    return w_uvqk_grad, w_out_grad, new_table, new_accum.reshape(own)


def solution(mesh):
    placed = (
        P("dp", None),
        P("dp", None),
        P("dp", None),
        P("dp"),
        P(None, "mp"),
        P("mp", None),
        P(("dp", "mp"), None),
        P(("dp", "mp")),
    )
    return jax.shard_map(
        body,
        mesh=mesh,
        in_specs=placed,
        out_specs=(P(None, "mp"), P("mp", None), P(("dp", "mp"), None), P(("dp", "mp"))),
        check_vma=False,
    )
```

```python
import functools

import jax
import jax.numpy as jnp
from jax import lax
from jax.experimental import pallas as pl
from jax.experimental.pallas import tpu as pltpu
from jax.sharding import PartitionSpec as P

HEAD_DIM = 64
BLOCK = 4 * HEAD_DIM
MESH = pl.DeviceIdType.MESH
F32, BF16 = jnp.float32, jnp.bfloat16

NN = (((1,), (0,)), ((), ()))
NT = (((1,), (1,)), ((), ()))
TN = (((0,), (0,)), ((), ()))


def halves(value):
    high = value.astype(BF16)
    return high, (value - high.astype(F32)).astype(BF16)


def dot(left, right, dims):
    return lax.dot_general(left, right, dims, preferred_element_type=F32)


def dot3(left, right, dims):
    return dot(left[0], right[1], dims) + dot(left[1], right[0], dims) + dot(left[0], right[0], dims)


def kernel(
    n_z, n_mp, fuse,
    x_hbm, g_hbm, seg_hbm, ids_hbm, w_hbm, wo_hbm, table_hbm, accum_ref,
    out_hbm, wopart_ref, newt_ref, newa_ref,
    x_ref, g_ref, seg_ref, ids_ref, w_ref, wo_ref, table_ref, in_sem, out_sem,
    out, buf, xt_hi, xt_lo, act, dsilu, attn, dsfac, outv, dzs, stat, stat_in,
    rc, rx, rz, sl, slc, slx, slz, slq, slm,
    ps, pr, zs, zr, ls, lr, lzs, lzr, ms, mr,
):
    loads = []
    for i, (src, dst) in enumerate((
        (seg_hbm, seg_ref), (x_hbm, x_ref), (w_hbm, w_ref), (g_hbm, g_ref),
        (wo_hbm, wo_ref), (ids_hbm, ids_ref), (table_hbm, table_ref),
    )):
        loads.append(pltpu.make_async_copy(src, dst, in_sem.at[i]))
        loads[-1].start()
    count, width = x_ref.shape
    heads = w_ref.shape[1] // BLOCK
    rows = sl.shape[0]
    own = table_ref.shape[0]
    off = 1 if fuse else 0
    pieces = heads + off
    half = buf.shape[1] // 2
    quarter = half // 2
    chunk = quarter // n_z
    scale = HEAD_DIM ** (-0.5)

    dp, mp = lax.axis_index("dp"), lax.axis_index("mp")
    z, x, c = dp // 4, (dp // 2) % 2, dp % 2
    at_core = {"dp": z * 4 + x * 2 + (1 - c)}
    at_x = {"dp": z * 4 + (1 - x) * 2 + c}
    z_of = [lax.rem(z + k, n_z) for k in range(1, n_z)]
    at_z = [{"dp": zz * 4 + x * 2 + c} for zz in z_of]
    at_mp = [{"mp": lax.rem(mp + k, n_mp)} for k in range(1, n_mp)]

    barrier = pltpu.get_barrier_semaphore()
    partners = [at_core, at_x] + at_z + at_mp
    for partner in partners:
        pl.semaphore_signal(barrier, inc=1, device_id=partner, device_id_type=MESH)

    def remote(src, dst, send, recv, where):
        return pltpu.make_async_remote_copy(
            src_ref=src, dst_ref=dst, send_sem=send, recv_sem=recv, device_id=where, device_id_type=MESH
        )

    def span(start, size):
        return pl.ds(pl.multiple_of(start, 8), size)

    mine = span(c * half, half)
    theirs = span((1 - c) * half, half)
    my_q = span(c * half + x * quarter, quarter)
    their_q = span(c * half + (1 - x) * quarter, quarter)
    my_chunk = span(c * half + x * quarter + z * chunk, chunk)

    def core_rs(p):
        return remote(buf.at[p, theirs], rc.at[p], ps.at[0, p], pr.at[0, p], at_core)

    def x_rs(p):
        return remote(buf.at[p, their_q], rx.at[p], ps.at[1, p], pr.at[1, p], at_x)

    def z_rs(p, k):
        part = span(c * half + x * quarter + z_of[k] * chunk, chunk)
        return remote(buf.at[p, part], rz.at[p, k], zs.at[0, p, k], zr.at[0, p, k], at_z[k])

    def z_ag(p, k):
        return remote(out.at[p, my_chunk], out.at[p, my_chunk], zs.at[1, p, k], zr.at[1, p, k], at_z[k])

    def x_ag(p):
        return remote(out.at[p, my_q], out.at[p, my_q], ps.at[2, p], pr.at[2, p], at_x)

    def core_ag(p):
        return remote(out.at[p, mine], out.at[p, mine], ps.at[3, p], pr.at[3, p], at_core)

    def keep(p):
        return pltpu.make_async_copy(out.at[p], out_hbm.at[p], out_sem.at[p])

    def stage(s, p):
        if s == 0:
            core_rs(p).start()
        elif s == 1:
            core_rs(p).wait()
            buf[p, their_q] += rc[p, span((1 - x) * quarter, quarter)]
            x_rs(p).start()
            buf[p, my_q] += rc[p, span(x * quarter, quarter)]
        elif s == 2:
            x_rs(p).wait()
            buf[p, my_q] += rx[p]
            for k in range(n_z - 1):
                z_rs(p, k).start()
        elif s == 3:
            total = buf[p, my_chunk]
            for k in range(n_z - 1):
                z_rs(p, k).wait()
                total = total + rz[p, k]
            out[p, my_chunk] = total
            for k in range(n_z - 1):
                z_ag(p, k).start()
        elif s == 4:
            for k in range(n_z - 1):
                z_ag(p, k).wait()
            x_ag(p).start()
        elif s == 5:
            x_ag(p).wait()
            core_ag(p).start()
        else:
            core_ag(p).wait()
            keep(p).start()

    loads[0].wait()
    seg = jnp.broadcast_to(seg_ref[...].astype(F32), (count, count))
    spot = lax.broadcasted_iota(jnp.int32, (count, count), 0)
    other = lax.broadcasted_iota(jnp.int32, (count, count), 1)
    mask = jnp.where((seg == seg.T) & (spot >= other), 1.0, 0.0)
    loads[1].wait()
    xs = halves(x_ref[...])
    loads[3].wait()
    gs = halves(g_ref[...])
    loads[2].wait()
    loads[4].wait()

    def forward(h, sums):
        ws = halves(w_ref[:, pl.ds(pl.multiple_of(h * BLOCK, BLOCK), BLOCK)])
        pre = dot3(xs, ws, NN)
        sig = jax.nn.sigmoid(pre)
        val = pre * sig
        act[h] = val
        dsilu[h] = sig * (1.0 + pre * (1.0 - sig))
        u, v = val[:, 0:64], val[:, 64:128]
        q, k = val[:, 128:192], val[:, 192:256]
        score = dot3(halves(q), halves(k), NT) * scale
        ssig = jax.nn.sigmoid(score)
        a = score * ssig * mask
        attn[h] = a
        dsfac[h] = mask * (ssig * (1.0 + score * (1.0 - ssig))) * scale
        o = dot3(halves(a), halves(v), NN)
        outv[h] = o
        wos = halves(wo_ref[pl.ds(pl.multiple_of(h * HEAD_DIM, HEAD_DIM), HEAD_DIM), :])
        dz = dot3(gs, wos, NT)
        dzs[h] = dz
        dn = dz * u
        return (sums[0] + o, sums[1] + o * o, sums[2] + dn, sums[3] + dn * o)

    zero = jnp.zeros((count, HEAD_DIM), F32)
    sums = lax.fori_loop(0, heads, forward, (zero, zero, zero, zero))
    lane = lax.broadcasted_iota(jnp.int32, (count, 128), 1)
    packed = jnp.zeros((count, 128), F32)
    for i in range(4):
        packed = jnp.where(lane == i, jnp.sum(sums[i], axis=1, keepdims=True), packed)
    stat[...] = packed.T[0:8]
    pl.semaphore_wait(barrier, len(partners))

    def stat_to(k):
        return remote(stat, stat_in.at[k], ms.at[0, k], mr.at[0, k], at_mp[k])

    for k in range(n_mp - 1):
        stat_to(k).start()
    loads[5].wait()
    loads[6].wait()
    x_t = x_ref[...].T
    xt_hi[...], xt_lo[...] = halves(x_t)
    place = lax.broadcasted_iota(jnp.int32, (rows, count), 0)
    inner = n_z * n_mp * own
    pc, px = place // (2 * inner), (place // inner) % 2
    pz, pm = (place // (n_mp * own)) % n_z, place % (n_mp * own)
    wanted = ((pz * 2 + px) * 2 + pc) * (n_mp * own) + pm
    hits = jnp.where(wanted == ids_ref[...], 1.0, 0.0).astype(BF16)
    sl[...] = (dot(hits, gs[0], NN) + dot(hits, gs[1], NN)) * (1.0 / n_mp)

    total = stat[...]
    for k in range(n_mp - 1):
        stat_to(k).wait()
        total = total + stat_in[k]
    cols = jnp.concatenate([total, jnp.zeros((120, count), F32)], axis=0).T
    mean = cols[:, 0:1] / width
    var = cols[:, 1:2] / width - mean * mean
    rstd = lax.rsqrt(var + 1e-05)
    m1 = cols[:, 2:3] / width
    m2 = rstd * (cols[:, 3:4] - mean * cols[:, 2:3]) / width

    z_all = jnp.concatenate(
        [(outv[h] - mean) * rstd * act[h][:, 0:64] for h in range(heads)], axis=1
    )
    wo_grad = dot3(halves(z_all), gs, TN)
    if fuse:
        buf[0, 0:half] = wo_grad[:, 0:BLOCK]
        buf[0, half : 2 * half] = wo_grad[:, BLOCK : 2 * BLOCK]
        stage(0, 0)
        wopart_ref[...] = jnp.zeros(wopart_ref.shape, F32)
    else:
        wopart_ref[...] = wo_grad

    def backward(h, carry):
        val = act[h]
        u, v = val[:, 0:64], val[:, 64:128]
        q, k = val[:, 128:192], val[:, 192:256]
        nrm = (outv[h] - mean) * rstd
        dz = dzs[h]
        dn = dz * u
        du = dz * nrm
        do = halves(rstd * (dn - m1 - nrm * m2))
        da = dot3(do, halves(v), NT)
        dv = dot3(halves(attn[h]), do, TN)
        ds = halves(da * dsfac[h])
        dq = dot3(ds, halves(k), NN)
        dk = dot3(ds, halves(q), TN)
        dpre = halves(jnp.concatenate([du, dv, dq, dk], axis=1) * dsilu[h])
        buf[h + off] = dot3((xt_hi[...], xt_lo[...]), dpre, NN)
        stage(0, h + off)
        rowsum = dot(hits, dpre[0], NN) + dot(hits, dpre[1], NN)
        ws = halves(w_ref[:, pl.ds(pl.multiple_of(h * BLOCK, BLOCK), BLOCK)])
        sl[...] += dot3(halves(rowsum), ws, NT)
        for s in range(1, min(6, heads - 1 + off) + 1):
            if off == 1 and s == 1:
                stage(s, h)
            else:
                pl.when(h + off - s >= 0)(functools.partial(stage, s, h + off - s))
        return carry

    lax.fori_loop(0, heads, backward, 0)

    s_half, s_q = rows // 2, rows // 4
    s_mine = span(c * s_half + x * s_q, s_q)

    def sl_core():
        return remote(sl.at[span((1 - c) * s_half, s_half)], slc, ls.at[0], lr.at[0], at_core)

    def sl_x():
        return remote(sl.at[span(c * s_half + (1 - x) * s_q, s_q)], slx, ls.at[1], lr.at[1], at_x)

    def sl_z(k):
        return remote(sl.at[s_mine], slz.at[k], lzs.at[k], lzr.at[k], at_z[k])

    def sl_mp(k):
        return remote(slq, slm.at[k], ms.at[1, k], mr.at[1, k], at_mp[k])

    def slab(t):
        if t == 0:
            sl_core().start()
        elif t == 1:
            sl_core().wait()
            sl[span(c * s_half, s_half)] += slc[...]
            sl_x().start()
        elif t == 2:
            sl_x().wait()
            sl[s_mine] += slx[...]
            for k in range(n_z - 1):
                sl_z(k).start()
        elif t == 3:
            part = sl[s_mine]
            for k in range(n_z - 1):
                sl_z(k).wait()
                part = part + slz[k]
            slq[...] = part
            for k in range(n_mp - 1):
                sl_mp(k).start()
        elif t == 4:
            part = slq[pl.ds((z * n_mp + mp) * own, own), :]
            for k in range(n_mp - 1):
                sl_mp(k).wait()
                part = part + slm[k, pl.ds((z * n_mp + mp) * own, own), :]
            newa = accum_ref[...] + jnp.sum(part * part, axis=1, keepdims=True) / width
            newa_ref[...] = newa
            newt_ref[...] = table_ref[...] - 0.5 * part * lax.rsqrt(newa)

    slab(0)
    for t in range(1, 7):
        tick = heads - 1 + off + t
        for s in range(0, 7):
            if 0 <= tick - s < pieces:
                stage(s, tick - s)
        slab(t)
    for p in range(pieces):
        keep(p).wait()


def layout_kernel(off, pieces_ref, table_ref, *refs):
    held, row, in_sem, sem = refs[-4:]
    w_ref, newt_ref = refs[0], refs[1]
    count = held.shape[0]
    loads = [pltpu.make_async_copy(pieces_ref.at[p], held.at[p], in_sem.at[p]) for p in range(count)]
    loads.append(pltpu.make_async_copy(table_ref, row, in_sem.at[count]))
    for load in loads:
        load.start()
    moves = []
    for p in range(count):
        if p < off:
            tokens = refs[2].shape[0]
            moves.append([
                (held.at[p, pl.ds(i * tokens, tokens)], refs[2].at[:, pl.ds(i * BLOCK, BLOCK)]) for i in range(2)
            ])
        else:
            moves.append([(held.at[p], w_ref.at[:, pl.ds((p - off) * BLOCK, BLOCK)])])
    moves.append([(row, newt_ref)])
    copies = []
    for load, after in zip(loads, moves):
        load.wait()
        for src, dst in after:
            copies.append(pltpu.make_async_copy(src, dst, sem.at[len(copies)]))
            copies[-1].start()
    for copy in copies:
        copy.wait()


def body(layer_input, grad_out, segment, item_ids, w_uvqk, w_out, table, accum):
    count, width = layer_input.shape
    cols = w_uvqk.shape[1]
    heads = cols // BLOCK
    feats = heads * HEAD_DIM
    n_dp, n_mp = lax.axis_size("dp"), lax.axis_size("mp")
    own = table.shape[0]
    rows = own * n_dp * n_mp
    n_z = n_dp // 4
    fuse = feats == BLOCK
    pieces = heads + (1 if fuse else 0)
    half, quarter = width // 2, width // 4
    chunk = quarter // n_z
    wo_shape = (8, 128) if fuse else (feats, width)
    vmem = pl.BlockSpec(memory_space=pltpu.VMEM)
    hbm = pl.BlockSpec(memory_space=pl.ANY)
    dma = pltpu.SemaphoreType.DMA
    out, wo_part, new_table, new_accum = pl.pallas_call(
        functools.partial(kernel, n_z, n_mp, fuse),
        out_shape=(
            jax.ShapeDtypeStruct((pieces, width, BLOCK), F32),
            jax.ShapeDtypeStruct(wo_shape, F32),
            jax.ShapeDtypeStruct((own, width), F32),
            jax.ShapeDtypeStruct((own, 1), F32),
        ),
        in_specs=[hbm] * 7 + [vmem],
        out_specs=(hbm, vmem, vmem, vmem),
        scratch_shapes=[
            pltpu.VMEM((count, width), F32),
            pltpu.VMEM((count, width), F32),
            pltpu.VMEM((1, count), jnp.int32),
            pltpu.VMEM((1, count), jnp.int32),
            pltpu.VMEM((width, cols), F32),
            pltpu.VMEM((feats, width), F32),
            pltpu.VMEM((own, width), F32),
            dma((7,)),
            dma((pieces,)),
            pltpu.VMEM((pieces, width, BLOCK), F32),
            pltpu.VMEM((pieces, width, BLOCK), F32),
            pltpu.VMEM((width, count), BF16),
            pltpu.VMEM((width, count), BF16),
            pltpu.VMEM((heads, count, BLOCK), F32),
            pltpu.VMEM((heads, count, BLOCK), F32),
            pltpu.VMEM((heads, count, count), F32),
            pltpu.VMEM((heads, count, count), F32),
            pltpu.VMEM((heads, count, HEAD_DIM), F32),
            pltpu.VMEM((heads, count, HEAD_DIM), F32),
            pltpu.VMEM((8, count), F32),
            pltpu.VMEM((n_mp - 1, 8, count), F32),
            pltpu.VMEM((pieces, half, BLOCK), F32),
            pltpu.VMEM((pieces, quarter, BLOCK), F32),
            pltpu.VMEM((pieces, n_z - 1, chunk, BLOCK), F32),
            pltpu.VMEM((rows, width), F32),
            pltpu.VMEM((rows // 2, width), F32),
            pltpu.VMEM((rows // 4, width), F32),
            pltpu.VMEM((n_z - 1, rows // 4, width), F32),
            pltpu.VMEM((rows // 4, width), F32),
            pltpu.VMEM((n_mp - 1, rows // 4, width), F32),
            dma((4, pieces)),
            dma((4, pieces)),
            dma((2, pieces, n_z - 1)),
            dma((2, pieces, n_z - 1)),
            dma((2,)),
            dma((2,)),
            dma((n_z - 1,)),
            dma((n_z - 1,)),
            dma((2, n_mp - 1)),
            dma((2, n_mp - 1)),
        ],
        compiler_params=pltpu.CompilerParams(
            collective_id=0, has_side_effects=True, vmem_limit_bytes=56 * 1024 * 1024
        ),
    )(
        layer_input,
        grad_out,
        segment,
        item_ids.reshape(1, count),
        w_uvqk,
        w_out,
        table,
        accum.reshape(own, 1),
    )
    results = [
        jax.ShapeDtypeStruct((width, cols), F32),
        jax.ShapeDtypeStruct((own, width), F32),
    ] + ([jax.ShapeDtypeStruct((feats, width), F32)] if fuse else [])
    laid = pl.pallas_call(
        functools.partial(layout_kernel, 1 if fuse else 0),
        out_shape=tuple(results),
        in_specs=[hbm] * 2,
        out_specs=(hbm,) * len(results),
        scratch_shapes=[
            pltpu.VMEM((pieces, width, BLOCK), F32),
            pltpu.VMEM((own, width), F32),
            dma((pieces + 1,)),
            dma((heads + 3,)),
        ],
        compiler_params=pltpu.CompilerParams(vmem_limit_bytes=56 * 1024 * 1024),
    )(out, new_table)
    w_uvqk_grad, new_table = laid[:2]
    w_out_grad = laid[2] if fuse else lax.psum(wo_part, "dp")
    return w_uvqk_grad, w_out_grad, new_table, new_accum.reshape(own)


def solution(mesh):
    placed = (
        P("dp", None),
        P("dp", None),
        P("dp", None),
        P("dp"),
        P(None, "mp"),
        P("mp", None),
        P(("dp", "mp"), None),
        P(("dp", "mp")),
    )
    return jax.shard_map(
        body,
        mesh=mesh,
        in_specs=placed,
        out_specs=(P(None, "mp"), P("mp", None), P(("dp", "mp"), None), P(("dp", "mp"))),
        check_vma=False,
    )
```

```python
import functools

import jax
import jax.numpy as jnp
from jax import lax
from jax.experimental import pallas as pl
from jax.experimental.pallas import tpu as pltpu
from jax.sharding import PartitionSpec as P

HEAD_DIM = 64
BLOCK = 4 * HEAD_DIM
MESH = pl.DeviceIdType.MESH
F32, BF16 = jnp.float32, jnp.bfloat16

NN = (((1,), (0,)), ((), ()))
NT = (((1,), (1,)), ((), ()))
TN = (((0,), (0,)), ((), ()))


def halves(value):
    high = value.astype(BF16)
    return high, (value - high.astype(F32)).astype(BF16)


def dot(left, right, dims):
    return lax.dot_general(left, right, dims, preferred_element_type=F32)


def dot3(left, right, dims):
    return dot(left[0], right[1], dims) + dot(left[1], right[0], dims) + dot(left[0], right[0], dims)


def kernel(
    n_z, n_mp, fuse,
    x_hbm, g_hbm, seg_hbm, ids_hbm, w_hbm, wo_hbm, table_hbm, accum_ref,
    out_hbm, wopart_ref, newt_ref, newa_ref,
    x_ref, g_ref, seg_ref, ids_ref, w_ref, wo_ref, table_ref, in_sem, out_sem,
    out, buf, xt_hi, xt_lo, act, dsilu, attn, dsfac, outv, dzs, stat, stat_in,
    rc, rx, rz, sl, slc, slx, slz, slq, slm,
    ps, pr, zs, zr, ls, lr, lzs, lzr, ms, mr,
):
    count, width = x_ref.shape
    heads = w_ref.shape[1] // BLOCK
    moves = [(seg_hbm, seg_ref), (x_hbm, x_ref)]
    for h in range(heads):
        at = pl.ds(h * BLOCK, BLOCK)
        moves.append((w_hbm.at[:, at], w_ref.at[:, at]))
    moves += [(g_hbm, g_ref), (wo_hbm, wo_ref), (ids_hbm, ids_ref), (table_hbm, table_ref)]
    loads = [pltpu.make_async_copy(src, dst, in_sem.at[i]) for i, (src, dst) in enumerate(moves)]
    for load in loads:
        load.start()
    w_loads = loads[2 : 2 + heads]
    loads = loads[:2] + loads[2 + heads :]
    rows = sl.shape[0]
    own = table_ref.shape[0]
    off = 1 if fuse else 0
    pieces = heads + off
    half = buf.shape[1] // 2
    quarter = half // 2
    chunk = quarter // n_z
    scale = HEAD_DIM ** (-0.5)

    dp, mp = lax.axis_index("dp"), lax.axis_index("mp")
    z, x, c = dp // 4, (dp // 2) % 2, dp % 2
    at_core = {"dp": z * 4 + x * 2 + (1 - c)}
    at_x = {"dp": z * 4 + (1 - x) * 2 + c}
    z_of = [lax.rem(z + k, n_z) for k in range(1, n_z)]
    at_z = [{"dp": zz * 4 + x * 2 + c} for zz in z_of]
    at_mp = [{"mp": lax.rem(mp + k, n_mp)} for k in range(1, n_mp)]

    barrier = pltpu.get_barrier_semaphore()
    partners = [at_core, at_x] + at_z + at_mp
    for partner in partners:
        pl.semaphore_signal(barrier, inc=1, device_id=partner, device_id_type=MESH)

    def remote(src, dst, send, recv, where):
        return pltpu.make_async_remote_copy(
            src_ref=src, dst_ref=dst, send_sem=send, recv_sem=recv, device_id=where, device_id_type=MESH
        )

    def span(start, size):
        return pl.ds(pl.multiple_of(start, 8), size)

    mine = span(c * half, half)
    theirs = span((1 - c) * half, half)
    my_q = span(c * half + x * quarter, quarter)
    their_q = span(c * half + (1 - x) * quarter, quarter)
    my_chunk = span(c * half + x * quarter + z * chunk, chunk)

    def core_rs(p):
        return remote(buf.at[p, theirs], rc.at[p], ps.at[0, p], pr.at[0, p], at_core)

    def x_rs(p):
        return remote(buf.at[p, their_q], rx.at[p], ps.at[1, p], pr.at[1, p], at_x)

    def z_rs(p, k):
        part = span(c * half + x * quarter + z_of[k] * chunk, chunk)
        return remote(buf.at[p, part], rz.at[p, k], zs.at[0, p, k], zr.at[0, p, k], at_z[k])

    def z_ag(p, k):
        return remote(out.at[p, my_chunk], out.at[p, my_chunk], zs.at[1, p, k], zr.at[1, p, k], at_z[k])

    def x_ag(p):
        return remote(out.at[p, my_q], out.at[p, my_q], ps.at[2, p], pr.at[2, p], at_x)

    def core_ag(p):
        return remote(out.at[p, mine], out.at[p, mine], ps.at[3, p], pr.at[3, p], at_core)

    def keep(p):
        return pltpu.make_async_copy(out.at[p], out_hbm.at[p], out_sem.at[p])

    def stage(s, p):
        if s == 0:
            core_rs(p).start()
        elif s == 1:
            core_rs(p).wait()
            buf[p, their_q] += rc[p, span((1 - x) * quarter, quarter)]
            x_rs(p).start()
            buf[p, my_q] += rc[p, span(x * quarter, quarter)]
        elif s == 2:
            x_rs(p).wait()
            buf[p, my_q] += rx[p]
            for k in range(n_z - 1):
                z_rs(p, k).start()
        elif s == 3:
            total = buf[p, my_chunk]
            for k in range(n_z - 1):
                z_rs(p, k).wait()
                total = total + rz[p, k]
            out[p, my_chunk] = total
            for k in range(n_z - 1):
                z_ag(p, k).start()
        elif s == 4:
            for k in range(n_z - 1):
                z_ag(p, k).wait()
            x_ag(p).start()
        elif s == 5:
            x_ag(p).wait()
            core_ag(p).start()
        else:
            core_ag(p).wait()
            keep(p).start()

    loads[0].wait()
    seg = jnp.broadcast_to(seg_ref[...].astype(F32), (count, count))
    spot = lax.broadcasted_iota(jnp.int32, (count, count), 0)
    other = lax.broadcasted_iota(jnp.int32, (count, count), 1)
    mask = jnp.where((seg == seg.T) & (spot >= other), 1.0, 0.0)
    loads[1].wait()
    xs = halves(x_ref[...])
    loads[2].wait()
    gs = halves(g_ref[...])
    loads[3].wait()

    def forward(h, sums):
        w_loads[h].wait()
        ws = halves(w_ref[:, h * BLOCK : (h + 1) * BLOCK])
        pre = dot3(xs, ws, NN)
        sig = jax.nn.sigmoid(pre)
        val = pre * sig
        act[h] = val
        dsilu[h] = sig * (1.0 + pre * (1.0 - sig))
        u, v = val[:, 0:64], val[:, 64:128]
        q, k = val[:, 128:192], val[:, 192:256]
        score = dot3(halves(q), halves(k), NT) * scale
        ssig = jax.nn.sigmoid(score)
        a = score * ssig * mask
        attn[h] = a
        dsfac[h] = mask * (ssig * (1.0 + score * (1.0 - ssig))) * scale
        o = dot3(halves(a), halves(v), NN)
        outv[h] = o
        wos = halves(wo_ref[h * HEAD_DIM : (h + 1) * HEAD_DIM, :])
        dz = dot3(gs, wos, NT)
        dzs[h] = dz
        dn = dz * u
        return (sums[0] + o, sums[1] + o * o, sums[2] + dn, sums[3] + dn * o)

    zero = jnp.zeros((count, HEAD_DIM), F32)
    sums = (zero, zero, zero, zero)
    for h in range(heads):
        sums = forward(h, sums)
    lane = lax.broadcasted_iota(jnp.int32, (count, 128), 1)
    packed = jnp.zeros((count, 128), F32)
    for i in range(4):
        packed = jnp.where(lane == i, jnp.sum(sums[i], axis=1, keepdims=True), packed)
    stat[...] = packed.T[0:8]
    pl.semaphore_wait(barrier, len(partners))

    def stat_to(k):
        return remote(stat, stat_in.at[k], ms.at[0, k], mr.at[0, k], at_mp[k])

    for k in range(n_mp - 1):
        stat_to(k).start()
    loads[4].wait()
    loads[5].wait()
    x_t = x_ref[...].T
    xt_hi[...], xt_lo[...] = halves(x_t)
    place = lax.broadcasted_iota(jnp.int32, (rows, count), 0)
    inner = n_z * n_mp * own
    pc, px = place // (2 * inner), (place // inner) % 2
    pz, pm = (place // (n_mp * own)) % n_z, place % (n_mp * own)
    wanted = ((pz * 2 + px) * 2 + pc) * (n_mp * own) + pm
    hits = jnp.where(wanted == ids_ref[...], 1.0, 0.0).astype(BF16)
    sl[...] = (dot(hits, gs[0], NN) + dot(hits, gs[1], NN)) * (1.0 / n_mp)

    total = stat[...]
    for k in range(n_mp - 1):
        stat_to(k).wait()
        total = total + stat_in[k]
    cols = jnp.concatenate([total, jnp.zeros((120, count), F32)], axis=0).T
    mean = cols[:, 0:1] / width
    var = cols[:, 1:2] / width - mean * mean
    rstd = lax.rsqrt(var + 1e-05)
    m1 = cols[:, 2:3] / width
    m2 = rstd * (cols[:, 3:4] - mean * cols[:, 2:3]) / width

    z_all = jnp.concatenate(
        [(outv[h] - mean) * rstd * act[h][:, 0:64] for h in range(heads)], axis=1
    )
    wo_grad = dot3(halves(z_all), gs, TN)
    if fuse:
        buf[0, 0:half] = wo_grad[:, 0:BLOCK]
        buf[0, half : 2 * half] = wo_grad[:, BLOCK : 2 * BLOCK]
        stage(0, 0)
        wopart_ref[...] = jnp.zeros(wopart_ref.shape, F32)
    else:
        wopart_ref[...] = wo_grad

    def backward(h, carry):
        val = act[h]
        u, v = val[:, 0:64], val[:, 64:128]
        q, k = val[:, 128:192], val[:, 192:256]
        nrm = (outv[h] - mean) * rstd
        dz = dzs[h]
        dn = dz * u
        du = dz * nrm
        do = halves(rstd * (dn - m1 - nrm * m2))
        da = dot3(do, halves(v), NT)
        dv = dot3(halves(attn[h]), do, TN)
        ds = halves(da * dsfac[h])
        dq = dot3(ds, halves(k), NN)
        dk = dot3(ds, halves(q), TN)
        dpre = halves(jnp.concatenate([du, dv, dq, dk], axis=1) * dsilu[h])
        buf[h + off] = dot3((xt_hi[...], xt_lo[...]), dpre, NN)
        stage(0, h + off)
        rowsum = dot(hits, dpre[0], NN) + dot(hits, dpre[1], NN)
        ws = halves(w_ref[:, pl.ds(pl.multiple_of(h * BLOCK, BLOCK), BLOCK)])
        sl[...] += dot3(halves(rowsum), ws, NT)
        for s in range(1, min(6, heads - 1 + off) + 1):
            if off == 1 and s == 1:
                stage(s, h)
            else:
                pl.when(h + off - s >= 0)(functools.partial(stage, s, h + off - s))
        return carry

    lax.fori_loop(0, heads, backward, 0)

    s_half, s_q = rows // 2, rows // 4
    s_mine = span(c * s_half + x * s_q, s_q)

    def sl_core():
        return remote(sl.at[span((1 - c) * s_half, s_half)], slc, ls.at[0], lr.at[0], at_core)

    def sl_x():
        return remote(sl.at[span(c * s_half + (1 - x) * s_q, s_q)], slx, ls.at[1], lr.at[1], at_x)

    def sl_z(k):
        return remote(sl.at[s_mine], slz.at[k], lzs.at[k], lzr.at[k], at_z[k])

    def sl_mp(k):
        return remote(slq, slm.at[k], ms.at[1, k], mr.at[1, k], at_mp[k])

    def slab(t):
        if t == 0:
            sl_core().start()
        elif t == 1:
            sl_core().wait()
            sl[span(c * s_half, s_half)] += slc[...]
            sl_x().start()
        elif t == 2:
            sl_x().wait()
            sl[s_mine] += slx[...]
            for k in range(n_z - 1):
                sl_z(k).start()
        elif t == 3:
            part = sl[s_mine]
            for k in range(n_z - 1):
                sl_z(k).wait()
                part = part + slz[k]
            slq[...] = part
            for k in range(n_mp - 1):
                sl_mp(k).start()
        elif t == 4:
            part = slq[pl.ds((z * n_mp + mp) * own, own), :]
            for k in range(n_mp - 1):
                sl_mp(k).wait()
                part = part + slm[k, pl.ds((z * n_mp + mp) * own, own), :]
            newa = accum_ref[...] + jnp.sum(part * part, axis=1, keepdims=True) / width
            newa_ref[...] = newa
            newt_ref[...] = table_ref[...] - 0.5 * part * lax.rsqrt(newa)

    slab(0)
    for t in range(1, 7):
        tick = heads - 1 + off + t
        for s in range(0, 7):
            if 0 <= tick - s < pieces:
                stage(s, tick - s)
        slab(t)
    for p in range(pieces):
        keep(p).wait()


def layout_kernel(off, pieces_ref, table_ref, *refs):
    held, row, in_sem, sem = refs[-4:]
    w_ref, newt_ref = refs[0], refs[1]
    count = held.shape[0]
    loads = [pltpu.make_async_copy(pieces_ref.at[p], held.at[p], in_sem.at[p]) for p in range(count)]
    loads.append(pltpu.make_async_copy(table_ref, row, in_sem.at[count]))
    for load in loads:
        load.start()
    moves = []
    for p in range(count):
        if p < off:
            tokens = refs[2].shape[0]
            moves.append([
                (held.at[p, pl.ds(i * tokens, tokens)], refs[2].at[:, pl.ds(i * BLOCK, BLOCK)]) for i in range(2)
            ])
        else:
            moves.append([(held.at[p], w_ref.at[:, pl.ds((p - off) * BLOCK, BLOCK)])])
    moves.append([(row, newt_ref)])
    copies = []
    for load, after in zip(loads, moves):
        load.wait()
        for src, dst in after:
            copies.append(pltpu.make_async_copy(src, dst, sem.at[len(copies)]))
            copies[-1].start()
    for copy in copies:
        copy.wait()


def body(layer_input, grad_out, segment, item_ids, w_uvqk, w_out, table, accum):
    count, width = layer_input.shape
    cols = w_uvqk.shape[1]
    heads = cols // BLOCK
    feats = heads * HEAD_DIM
    n_dp, n_mp = lax.axis_size("dp"), lax.axis_size("mp")
    own = table.shape[0]
    rows = own * n_dp * n_mp
    n_z = n_dp // 4
    fuse = feats == BLOCK
    pieces = heads + (1 if fuse else 0)
    half, quarter = width // 2, width // 4
    chunk = quarter // n_z
    wo_shape = (8, 128) if fuse else (feats, width)
    vmem = pl.BlockSpec(memory_space=pltpu.VMEM)
    hbm = pl.BlockSpec(memory_space=pl.ANY)
    dma = pltpu.SemaphoreType.DMA
    out, wo_part, new_table, new_accum = pl.pallas_call(
        functools.partial(kernel, n_z, n_mp, fuse),
        out_shape=(
            jax.ShapeDtypeStruct((pieces, width, BLOCK), F32),
            jax.ShapeDtypeStruct(wo_shape, F32),
            jax.ShapeDtypeStruct((own, width), F32),
            jax.ShapeDtypeStruct((own, 1), F32),
        ),
        in_specs=[hbm] * 7 + [vmem],
        out_specs=(hbm, vmem, vmem, vmem),
        scratch_shapes=[
            pltpu.VMEM((count, width), F32),
            pltpu.VMEM((count, width), F32),
            pltpu.VMEM((1, count), jnp.int32),
            pltpu.VMEM((1, count), jnp.int32),
            pltpu.VMEM((width, cols), F32),
            pltpu.VMEM((feats, width), F32),
            pltpu.VMEM((own, width), F32),
            dma((heads + 6,)),
            dma((pieces,)),
            pltpu.VMEM((pieces, width, BLOCK), F32),
            pltpu.VMEM((pieces, width, BLOCK), F32),
            pltpu.VMEM((width, count), BF16),
            pltpu.VMEM((width, count), BF16),
            pltpu.VMEM((heads, count, BLOCK), F32),
            pltpu.VMEM((heads, count, BLOCK), F32),
            pltpu.VMEM((heads, count, count), F32),
            pltpu.VMEM((heads, count, count), F32),
            pltpu.VMEM((heads, count, HEAD_DIM), F32),
            pltpu.VMEM((heads, count, HEAD_DIM), F32),
            pltpu.VMEM((8, count), F32),
            pltpu.VMEM((n_mp - 1, 8, count), F32),
            pltpu.VMEM((pieces, half, BLOCK), F32),
            pltpu.VMEM((pieces, quarter, BLOCK), F32),
            pltpu.VMEM((pieces, n_z - 1, chunk, BLOCK), F32),
            pltpu.VMEM((rows, width), F32),
            pltpu.VMEM((rows // 2, width), F32),
            pltpu.VMEM((rows // 4, width), F32),
            pltpu.VMEM((n_z - 1, rows // 4, width), F32),
            pltpu.VMEM((rows // 4, width), F32),
            pltpu.VMEM((n_mp - 1, rows // 4, width), F32),
            dma((4, pieces)),
            dma((4, pieces)),
            dma((2, pieces, n_z - 1)),
            dma((2, pieces, n_z - 1)),
            dma((2,)),
            dma((2,)),
            dma((n_z - 1,)),
            dma((n_z - 1,)),
            dma((2, n_mp - 1)),
            dma((2, n_mp - 1)),
        ],
        compiler_params=pltpu.CompilerParams(
            collective_id=0, has_side_effects=True, vmem_limit_bytes=56 * 1024 * 1024
        ),
    )(
        layer_input,
        grad_out,
        segment,
        item_ids.reshape(1, count),
        w_uvqk,
        w_out,
        table,
        accum.reshape(own, 1),
    )
    results = [
        jax.ShapeDtypeStruct((width, cols), F32),
        jax.ShapeDtypeStruct((own, width), F32),
    ] + ([jax.ShapeDtypeStruct((feats, width), F32)] if fuse else [])
    laid = pl.pallas_call(
        functools.partial(layout_kernel, 1 if fuse else 0),
        out_shape=tuple(results),
        in_specs=[hbm] * 2,
        out_specs=(hbm,) * len(results),
        scratch_shapes=[
            pltpu.VMEM((pieces, width, BLOCK), F32),
            pltpu.VMEM((own, width), F32),
            dma((pieces + 1,)),
            dma((heads + 3,)),
        ],
        compiler_params=pltpu.CompilerParams(vmem_limit_bytes=56 * 1024 * 1024),
    )(out, new_table)
    w_uvqk_grad, new_table = laid[:2]
    w_out_grad = laid[2] if fuse else lax.psum(wo_part, "dp")
    return w_uvqk_grad, w_out_grad, new_table, new_accum.reshape(own)


def solution(mesh):
    placed = (
        P("dp", None),
        P("dp", None),
        P("dp", None),
        P("dp"),
        P(None, "mp"),
        P("mp", None),
        P(("dp", "mp"), None),
        P(("dp", "mp")),
    )
    return jax.shard_map(
        body,
        mesh=mesh,
        in_specs=placed,
        out_specs=(P(None, "mp"), P("mp", None), P(("dp", "mp"), None), P(("dp", "mp"))),
        check_vma=False,
    )
```

```python
import functools

import jax
import jax.numpy as jnp
from jax import lax
from jax.experimental import pallas as pl
from jax.experimental.pallas import tpu as pltpu
from jax.sharding import PartitionSpec as P

HEAD_DIM = 64
BLOCK = 4 * HEAD_DIM
ORDER = (0, 1, 3, 4, 2, 5, 6)
MESH = pl.DeviceIdType.MESH
F32, BF16 = jnp.float32, jnp.bfloat16

NN = (((1,), (0,)), ((), ()))
NT = (((1,), (1,)), ((), ()))
TN = (((0,), (0,)), ((), ()))


def halves(value):
    high = value.astype(BF16)
    return high, (value - high.astype(F32)).astype(BF16)


def dot(left, right, dims):
    return lax.dot_general(left, right, dims, preferred_element_type=F32)


def dot3(left, right, dims):
    return dot(left[0], right[1], dims) + dot(left[1], right[0], dims) + dot(left[0], right[0], dims)


def kernel(
    n_z, n_mp, fuse,
    x_hbm, g_hbm, seg_hbm, ids_hbm, w_hbm, wo_hbm, table_hbm, accum_ref,
    out_hbm, wopart_ref, newt_ref, newa_ref,
    x_ref, g_ref, seg_ref, ids_ref, w_ref, wo_ref, table_ref, in_sem, out_sem,
    out, buf, xt_hi, xt_lo, act, dsilu, attn, dsfac, outv, dzs, stat, stat_in,
    rc, rx, rz, sl, slc, slx, slz, slq, slm,
    ps, pr, zs, zr, ls, lr, lzs, lzr, ms, mr,
):
    loads = []
    for i, (src, dst) in enumerate((
        (seg_hbm, seg_ref), (x_hbm, x_ref), (w_hbm, w_ref), (g_hbm, g_ref),
        (wo_hbm, wo_ref), (ids_hbm, ids_ref), (table_hbm, table_ref),
    )):
        loads.append(pltpu.make_async_copy(src, dst, in_sem.at[i]))
        loads[-1].start()
    count, width = x_ref.shape
    heads = w_ref.shape[1] // BLOCK
    rows = sl.shape[0]
    own = table_ref.shape[0]
    off = 1 if fuse else 0
    pieces = heads + off
    half = buf.shape[1] // 2
    quarter = half // 2
    chunk = quarter // n_z
    scale = HEAD_DIM ** (-0.5)

    dp, mp = lax.axis_index("dp"), lax.axis_index("mp")
    z, x, c = dp // 4, (dp // 2) % 2, dp % 2
    at_core = {"dp": z * 4 + x * 2 + (1 - c)}
    at_x = {"dp": z * 4 + (1 - x) * 2 + c}
    z_of = [lax.rem(z + k, n_z) for k in range(1, n_z)]
    at_z = [{"dp": zz * 4 + x * 2 + c} for zz in z_of]
    at_mp = [{"mp": lax.rem(mp + k, n_mp)} for k in range(1, n_mp)]

    barrier = pltpu.get_barrier_semaphore()
    partners = [at_core, at_x] + at_z + at_mp
    for partner in partners:
        pl.semaphore_signal(barrier, inc=1, device_id=partner, device_id_type=MESH)

    def remote(src, dst, send, recv, where):
        return pltpu.make_async_remote_copy(
            src_ref=src, dst_ref=dst, send_sem=send, recv_sem=recv, device_id=where, device_id_type=MESH
        )

    def span(start, size):
        return pl.ds(pl.multiple_of(start, 8), size)

    mine = span(c * half, half)
    theirs = span((1 - c) * half, half)
    my_q = span(c * half + x * quarter, quarter)
    their_q = span(c * half + (1 - x) * quarter, quarter)
    my_chunk = span(c * half + x * quarter + z * chunk, chunk)

    def core_rs(p):
        return remote(buf.at[p, theirs], rc.at[p], ps.at[0, p], pr.at[0, p], at_core)

    def x_rs(p):
        return remote(buf.at[p, their_q], rx.at[p], ps.at[1, p], pr.at[1, p], at_x)

    def z_rs(p, k):
        part = span(c * half + x * quarter + z_of[k] * chunk, chunk)
        return remote(buf.at[p, part], rz.at[p, k], zs.at[0, p, k], zr.at[0, p, k], at_z[k])

    def z_ag(p, k):
        return remote(out.at[p, my_chunk], out.at[p, my_chunk], zs.at[1, p, k], zr.at[1, p, k], at_z[k])

    def x_ag(p):
        return remote(out.at[p, my_q], out.at[p, my_q], ps.at[2, p], pr.at[2, p], at_x)

    def core_ag(p):
        return remote(out.at[p, mine], out.at[p, mine], ps.at[3, p], pr.at[3, p], at_core)

    def keep(p):
        return pltpu.make_async_copy(out.at[p], out_hbm.at[p], out_sem.at[p])

    def stage(s, p):
        if s == 0:
            core_rs(p).start()
        elif s == 1:
            core_rs(p).wait()
            buf[p, their_q] += rc[p, span((1 - x) * quarter, quarter)]
            x_rs(p).start()
            buf[p, my_q] += rc[p, span(x * quarter, quarter)]
        elif s == 2:
            x_rs(p).wait()
            buf[p, my_q] += rx[p]
            for k in range(n_z - 1):
                z_rs(p, k).start()
        elif s == 3:
            total = buf[p, my_chunk]
            for k in range(n_z - 1):
                z_rs(p, k).wait()
                total = total + rz[p, k]
            out[p, my_chunk] = total
            for k in range(n_z - 1):
                z_ag(p, k).start()
        elif s == 4:
            for k in range(n_z - 1):
                z_ag(p, k).wait()
            x_ag(p).start()
        elif s == 5:
            x_ag(p).wait()
            core_ag(p).start()
        else:
            core_ag(p).wait()
            keep(p).start()

    loads[0].wait()
    seg = jnp.broadcast_to(seg_ref[...].astype(F32), (count, count))
    spot = lax.broadcasted_iota(jnp.int32, (count, count), 0)
    other = lax.broadcasted_iota(jnp.int32, (count, count), 1)
    mask = jnp.where((seg == seg.T) & (spot >= other), 1.0, 0.0)
    loads[1].wait()
    xs = halves(x_ref[...])
    loads[3].wait()
    gs = halves(g_ref[...])
    loads[2].wait()
    loads[4].wait()

    def forward(h, sums):
        ws = halves(w_ref[:, pl.ds(pl.multiple_of(h * BLOCK, BLOCK), BLOCK)])
        pre = dot3(xs, ws, NN)
        sig = jax.nn.sigmoid(pre)
        val = pre * sig
        act[h] = val
        dsilu[h] = sig * (1.0 + pre * (1.0 - sig))
        u, v = val[:, 0:64], val[:, 64:128]
        q, k = val[:, 128:192], val[:, 192:256]
        score = dot3(halves(q), halves(k), NT) * scale
        ssig = jax.nn.sigmoid(score)
        a = score * ssig * mask
        attn[h] = a
        dsfac[h] = mask * (ssig * (1.0 + score * (1.0 - ssig))) * scale
        o = dot3(halves(a), halves(v), NN)
        outv[h] = o
        wos = halves(wo_ref[pl.ds(pl.multiple_of(h * HEAD_DIM, HEAD_DIM), HEAD_DIM), :])
        dz = dot3(gs, wos, NT)
        dzs[h] = dz
        dn = dz * u
        return (sums[0] + o, sums[1] + o * o, sums[2] + dn, sums[3] + dn * o)

    zero = jnp.zeros((count, HEAD_DIM), F32)
    sums = lax.fori_loop(0, heads, forward, (zero, zero, zero, zero))
    lane = lax.broadcasted_iota(jnp.int32, (count, 128), 1)
    packed = jnp.zeros((count, 128), F32)
    for i in range(4):
        packed = jnp.where(lane == i, jnp.sum(sums[i], axis=1, keepdims=True), packed)
    stat[...] = packed.T[0:8]
    pl.semaphore_wait(barrier, len(partners))

    def stat_to(k):
        return remote(stat, stat_in.at[k], ms.at[0, k], mr.at[0, k], at_mp[k])

    for k in range(n_mp - 1):
        stat_to(k).start()
    loads[5].wait()
    loads[6].wait()
    x_t = x_ref[...].T
    xt_hi[...], xt_lo[...] = halves(x_t)
    place = lax.broadcasted_iota(jnp.int32, (rows, count), 0)
    inner = n_z * n_mp * own
    pc, px = place // (2 * inner), (place // inner) % 2
    pz, pm = (place // (n_mp * own)) % n_z, place % (n_mp * own)
    wanted = ((pz * 2 + px) * 2 + pc) * (n_mp * own) + pm
    hits = jnp.where(wanted == ids_ref[...], 1.0, 0.0).astype(BF16)
    sl[...] = (dot(hits, gs[0], NN) + dot(hits, gs[1], NN)) * (1.0 / n_mp)

    total = stat[...]
    for k in range(n_mp - 1):
        stat_to(k).wait()
        total = total + stat_in[k]
    cols = jnp.concatenate([total, jnp.zeros((120, count), F32)], axis=0).T
    mean = cols[:, 0:1] / width
    var = cols[:, 1:2] / width - mean * mean
    rstd = lax.rsqrt(var + 1e-05)
    m1 = cols[:, 2:3] / width
    m2 = rstd * (cols[:, 3:4] - mean * cols[:, 2:3]) / width

    z_all = jnp.concatenate(
        [(outv[h] - mean) * rstd * act[h][:, 0:64] for h in range(heads)], axis=1
    )
    wo_grad = dot3(halves(z_all), gs, TN)
    if fuse:
        buf[0, 0:half] = wo_grad[:, 0:BLOCK]
        buf[0, half : 2 * half] = wo_grad[:, BLOCK : 2 * BLOCK]
        stage(0, 0)
        wopart_ref[...] = jnp.zeros(wopart_ref.shape, F32)
    else:
        wopart_ref[...] = wo_grad

    def backward(h, carry):
        val = act[h]
        u, v = val[:, 0:64], val[:, 64:128]
        q, k = val[:, 128:192], val[:, 192:256]
        nrm = (outv[h] - mean) * rstd
        dz = dzs[h]
        dn = dz * u
        du = dz * nrm
        do = halves(rstd * (dn - m1 - nrm * m2))
        da = dot3(do, halves(v), NT)
        dv = dot3(halves(attn[h]), do, TN)
        ds = halves(da * dsfac[h])
        dq = dot3(ds, halves(k), NN)
        dk = dot3(ds, halves(q), TN)
        dpre = halves(jnp.concatenate([du, dv, dq, dk], axis=1) * dsilu[h])
        buf[h + off] = dot3((xt_hi[...], xt_lo[...]), dpre, NN)
        stage(0, h + off)
        rowsum = dot(hits, dpre[0], NN) + dot(hits, dpre[1], NN)
        ws = halves(w_ref[:, pl.ds(pl.multiple_of(h * BLOCK, BLOCK), BLOCK)])
        sl[...] += dot3(halves(rowsum), ws, NT)
        for s in [s for s in ORDER if 1 <= s <= heads - 1 + off]:
            if off == 1 and s == 1:
                stage(s, h)
            else:
                pl.when(h + off - s >= 0)(functools.partial(stage, s, h + off - s))
        return carry

    lax.fori_loop(0, heads, backward, 0)

    s_half, s_q = rows // 2, rows // 4
    s_mine = span(c * s_half + x * s_q, s_q)

    def sl_core():
        return remote(sl.at[span((1 - c) * s_half, s_half)], slc, ls.at[0], lr.at[0], at_core)

    def sl_x():
        return remote(sl.at[span(c * s_half + (1 - x) * s_q, s_q)], slx, ls.at[1], lr.at[1], at_x)

    def sl_z(k):
        return remote(sl.at[s_mine], slz.at[k], lzs.at[k], lzr.at[k], at_z[k])

    def sl_mp(k):
        return remote(slq, slm.at[k], ms.at[1, k], mr.at[1, k], at_mp[k])

    def slab(t):
        if t == 0:
            sl_core().start()
        elif t == 1:
            sl_core().wait()
            sl[span(c * s_half, s_half)] += slc[...]
            sl_x().start()
        elif t == 2:
            sl_x().wait()
            sl[s_mine] += slx[...]
            for k in range(n_z - 1):
                sl_z(k).start()
        elif t == 3:
            part = sl[s_mine]
            for k in range(n_z - 1):
                sl_z(k).wait()
                part = part + slz[k]
            slq[...] = part
            for k in range(n_mp - 1):
                sl_mp(k).start()
        elif t == 4:
            part = slq[pl.ds((z * n_mp + mp) * own, own), :]
            for k in range(n_mp - 1):
                sl_mp(k).wait()
                part = part + slm[k, pl.ds((z * n_mp + mp) * own, own), :]
            newa = accum_ref[...] + jnp.sum(part * part, axis=1, keepdims=True) / width
            newa_ref[...] = newa
            newt_ref[...] = table_ref[...] - 0.5 * part * lax.rsqrt(newa)

    slab(0)
    for t in range(1, 7):
        tick = heads - 1 + off + t
        for s in ORDER:
            if 0 <= tick - s < pieces:
                stage(s, tick - s)
        slab(t)
    for p in range(pieces):
        keep(p).wait()


def layout_kernel(off, pieces_ref, table_ref, *refs):
    held, row, in_sem, sem = refs[-4:]
    w_ref, newt_ref = refs[0], refs[1]
    count = held.shape[0]
    loads = [pltpu.make_async_copy(pieces_ref.at[p], held.at[p], in_sem.at[p]) for p in range(count)]
    loads.append(pltpu.make_async_copy(table_ref, row, in_sem.at[count]))
    for load in loads:
        load.start()
    moves = []
    for p in range(count):
        if p < off:
            tokens = refs[2].shape[0]
            moves.append([
                (held.at[p, pl.ds(i * tokens, tokens)], refs[2].at[:, pl.ds(i * BLOCK, BLOCK)]) for i in range(2)
            ])
        else:
            moves.append([(held.at[p], w_ref.at[:, pl.ds((p - off) * BLOCK, BLOCK)])])
    moves.append([(row, newt_ref)])
    copies = []
    for load, after in zip(loads, moves):
        load.wait()
        for src, dst in after:
            copies.append(pltpu.make_async_copy(src, dst, sem.at[len(copies)]))
            copies[-1].start()
    for copy in copies:
        copy.wait()


def body(layer_input, grad_out, segment, item_ids, w_uvqk, w_out, table, accum):
    count, width = layer_input.shape
    cols = w_uvqk.shape[1]
    heads = cols // BLOCK
    feats = heads * HEAD_DIM
    n_dp, n_mp = lax.axis_size("dp"), lax.axis_size("mp")
    own = table.shape[0]
    rows = own * n_dp * n_mp
    n_z = n_dp // 4
    fuse = feats == BLOCK
    pieces = heads + (1 if fuse else 0)
    half, quarter = width // 2, width // 4
    chunk = quarter // n_z
    wo_shape = (8, 128) if fuse else (feats, width)
    vmem = pl.BlockSpec(memory_space=pltpu.VMEM)
    hbm = pl.BlockSpec(memory_space=pl.ANY)
    dma = pltpu.SemaphoreType.DMA
    out, wo_part, new_table, new_accum = pl.pallas_call(
        functools.partial(kernel, n_z, n_mp, fuse),
        out_shape=(
            jax.ShapeDtypeStruct((pieces, width, BLOCK), F32),
            jax.ShapeDtypeStruct(wo_shape, F32),
            jax.ShapeDtypeStruct((own, width), F32),
            jax.ShapeDtypeStruct((own, 1), F32),
        ),
        in_specs=[hbm] * 7 + [vmem],
        out_specs=(hbm, vmem, vmem, vmem),
        scratch_shapes=[
            pltpu.VMEM((count, width), F32),
            pltpu.VMEM((count, width), F32),
            pltpu.VMEM((1, count), jnp.int32),
            pltpu.VMEM((1, count), jnp.int32),
            pltpu.VMEM((width, cols), F32),
            pltpu.VMEM((feats, width), F32),
            pltpu.VMEM((own, width), F32),
            dma((7,)),
            dma((pieces,)),
            pltpu.VMEM((pieces, width, BLOCK), F32),
            pltpu.VMEM((pieces, width, BLOCK), F32),
            pltpu.VMEM((width, count), BF16),
            pltpu.VMEM((width, count), BF16),
            pltpu.VMEM((heads, count, BLOCK), F32),
            pltpu.VMEM((heads, count, BLOCK), F32),
            pltpu.VMEM((heads, count, count), F32),
            pltpu.VMEM((heads, count, count), F32),
            pltpu.VMEM((heads, count, HEAD_DIM), F32),
            pltpu.VMEM((heads, count, HEAD_DIM), F32),
            pltpu.VMEM((8, count), F32),
            pltpu.VMEM((n_mp - 1, 8, count), F32),
            pltpu.VMEM((pieces, half, BLOCK), F32),
            pltpu.VMEM((pieces, quarter, BLOCK), F32),
            pltpu.VMEM((pieces, n_z - 1, chunk, BLOCK), F32),
            pltpu.VMEM((rows, width), F32),
            pltpu.VMEM((rows // 2, width), F32),
            pltpu.VMEM((rows // 4, width), F32),
            pltpu.VMEM((n_z - 1, rows // 4, width), F32),
            pltpu.VMEM((rows // 4, width), F32),
            pltpu.VMEM((n_mp - 1, rows // 4, width), F32),
            dma((4, pieces)),
            dma((4, pieces)),
            dma((2, pieces, n_z - 1)),
            dma((2, pieces, n_z - 1)),
            dma((2,)),
            dma((2,)),
            dma((n_z - 1,)),
            dma((n_z - 1,)),
            dma((2, n_mp - 1)),
            dma((2, n_mp - 1)),
        ],
        compiler_params=pltpu.CompilerParams(
            collective_id=0, has_side_effects=True, vmem_limit_bytes=56 * 1024 * 1024
        ),
    )(
        layer_input,
        grad_out,
        segment,
        item_ids.reshape(1, count),
        w_uvqk,
        w_out,
        table,
        accum.reshape(own, 1),
    )
    results = [
        jax.ShapeDtypeStruct((width, cols), F32),
        jax.ShapeDtypeStruct((own, width), F32),
    ] + ([jax.ShapeDtypeStruct((feats, width), F32)] if fuse else [])
    laid = pl.pallas_call(
        functools.partial(layout_kernel, 1 if fuse else 0),
        out_shape=tuple(results),
        in_specs=[hbm] * 2,
        out_specs=(hbm,) * len(results),
        scratch_shapes=[
            pltpu.VMEM((pieces, width, BLOCK), F32),
            pltpu.VMEM((own, width), F32),
            dma((pieces + 1,)),
            dma((heads + 3,)),
        ],
        compiler_params=pltpu.CompilerParams(vmem_limit_bytes=56 * 1024 * 1024),
    )(out, new_table)
    w_uvqk_grad, new_table = laid[:2]
    w_out_grad = laid[2] if fuse else lax.psum(wo_part, "dp")
    return w_uvqk_grad, w_out_grad, new_table, new_accum.reshape(own)


def solution(mesh):
    placed = (
        P("dp", None),
        P("dp", None),
        P("dp", None),
        P("dp"),
        P(None, "mp"),
        P("mp", None),
        P(("dp", "mp"), None),
        P(("dp", "mp")),
    )
    return jax.shard_map(
        body,
        mesh=mesh,
        in_specs=placed,
        out_specs=(P(None, "mp"), P("mp", None), P(("dp", "mp"), None), P(("dp", "mp"))),
        check_vma=False,
    )
```

```python
import functools

import jax
import jax.numpy as jnp
from jax import lax
from jax.experimental import pallas as pl
from jax.experimental.pallas import tpu as pltpu
from jax.sharding import PartitionSpec as P

HEAD_DIM = 64
BLOCK = 4 * HEAD_DIM
MESH = pl.DeviceIdType.MESH
F32, BF16 = jnp.float32, jnp.bfloat16

NN = (((1,), (0,)), ((), ()))
NT = (((1,), (1,)), ((), ()))
TN = (((0,), (0,)), ((), ()))


def halves(value):
    high = value.astype(BF16)
    return high, (value - high.astype(F32)).astype(BF16)


def dot(left, right, dims):
    return lax.dot_general(left, right, dims, preferred_element_type=F32)


def dot3(left, right, dims):
    return dot(left[0], right[1], dims) + dot(left[1], right[0], dims) + dot(left[0], right[0], dims)


def kernel(
    n_z, n_mp, fuse,
    x_hbm, g_hbm, seg_hbm, ids_hbm, w_hbm, wo_hbm, table_hbm, accum_ref,
    out_hbm, wopart_ref, newt_ref, newa_ref,
    x_ref, g_ref, seg_ref, ids_ref, w_ref, wo_ref, table_ref, in_sem, out_sem,
    out, buf, xt_hi, xt_lo, act, dsilu, attn, dsfac, outv, dzs, stat, stat_in,
    rc, rx, rz, sl, slc, slx, slz, slq, slm,
    ps, pr, x_send, x_recv, zs, zr, ls, lr, lzs, lzr, ms, mr,
):
    loads = []
    for i, (src, dst) in enumerate((
        (seg_hbm, seg_ref), (x_hbm, x_ref), (w_hbm, w_ref), (g_hbm, g_ref),
        (wo_hbm, wo_ref), (ids_hbm, ids_ref), (table_hbm, table_ref),
    )):
        loads.append(pltpu.make_async_copy(src, dst, in_sem.at[i]))
        loads[-1].start()
    count, width = x_ref.shape
    heads = w_ref.shape[1] // BLOCK
    rows = sl.shape[0]
    own = table_ref.shape[0]
    off = 1 if fuse else 0
    pieces = heads + off
    half = buf.shape[1] // 2
    quarter = half // 2
    chunk = quarter // n_z
    scale = HEAD_DIM ** (-0.5)

    dp, mp = lax.axis_index("dp"), lax.axis_index("mp")
    z, x, c = dp // 4, (dp // 2) % 2, dp % 2
    at_core = {"dp": z * 4 + x * 2 + (1 - c)}
    at_x = {"dp": z * 4 + (1 - x) * 2 + c}
    z_of = [lax.rem(z + k, n_z) for k in range(1, n_z)]
    at_z = [{"dp": zz * 4 + x * 2 + c} for zz in z_of]
    at_mp = [{"mp": lax.rem(mp + k, n_mp)} for k in range(1, n_mp)]

    barrier = pltpu.get_barrier_semaphore()
    partners = [at_core, at_x] + at_z + at_mp
    for partner in partners:
        pl.semaphore_signal(barrier, inc=1, device_id=partner, device_id_type=MESH)

    def remote(src, dst, send, recv, where):
        return pltpu.make_async_remote_copy(
            src_ref=src, dst_ref=dst, send_sem=send, recv_sem=recv, device_id=where, device_id_type=MESH
        )

    def span(start, size):
        return pl.ds(pl.multiple_of(start, 8), size)

    mine = span(c * half, half)
    theirs = span((1 - c) * half, half)
    my_q = span(c * half + x * quarter, quarter)
    their_q = span(c * half + (1 - x) * quarter, quarter)
    my_chunk = span(c * half + x * quarter + z * chunk, chunk)

    def core_rs(p):
        return remote(buf.at[p, theirs], rc.at[p], ps.at[0, p], pr.at[0, p], at_core)

    def x_rs(p):
        return remote(buf.at[p, their_q], rx.at[p], ps.at[1, p], pr.at[1, p], at_x)

    def z_rs(p, k):
        part = span(c * half + x * quarter + z_of[k] * chunk, chunk)
        return remote(buf.at[p, part], rz.at[p, k], zs.at[0, p, k], zr.at[0, p, k], at_z[k])

    def z_ag(p, k):
        return remote(out.at[p, my_chunk], out.at[p, my_chunk], zs.at[1, p, k], zr.at[1, p, k], at_z[k])

    def x_ag(p, k):
        at = span(c * half + x * quarter + lax.rem(z - k + n_z, n_z) * chunk, chunk)
        return remote(out.at[p, at], out.at[p, at], x_send.at[p, k], x_recv.at[p, k], at_x)

    def core_ag(p):
        return remote(out.at[p, mine], out.at[p, mine], ps.at[3, p], pr.at[3, p], at_core)

    def keep(p):
        return pltpu.make_async_copy(out.at[p], out_hbm.at[p], out_sem.at[p])

    def stage(s, p):
        if s == 0:
            core_rs(p).start()
        elif s == 1:
            core_rs(p).wait()
            buf[p, their_q] += rc[p, span((1 - x) * quarter, quarter)]
            x_rs(p).start()
            buf[p, my_q] += rc[p, span(x * quarter, quarter)]
        elif s == 2:
            x_rs(p).wait()
            buf[p, my_q] += rx[p]
            for k in range(n_z - 1):
                z_rs(p, k).start()
        elif s == 3:
            total = buf[p, my_chunk]
            for k in range(n_z - 1):
                z_rs(p, k).wait()
                total = total + rz[p, k]
            out[p, my_chunk] = total
            for k in range(n_z - 1):
                z_ag(p, k).start()
            x_ag(p, 0).start()
        elif s == 4:
            for k in range(n_z - 1):
                z_ag(p, k).wait()
                x_ag(p, k + 1).start()
        elif s == 5:
            for k in range(n_z):
                x_ag(p, k).wait()
            core_ag(p).start()
        else:
            core_ag(p).wait()
            keep(p).start()

    loads[0].wait()
    seg = jnp.broadcast_to(seg_ref[...].astype(F32), (count, count))
    spot = lax.broadcasted_iota(jnp.int32, (count, count), 0)
    other = lax.broadcasted_iota(jnp.int32, (count, count), 1)
    mask = jnp.where((seg == seg.T) & (spot >= other), 1.0, 0.0)
    loads[1].wait()
    xs = halves(x_ref[...])
    loads[3].wait()
    gs = halves(g_ref[...])
    loads[2].wait()
    loads[4].wait()

    def forward(h, sums):
        ws = halves(w_ref[:, pl.ds(pl.multiple_of(h * BLOCK, BLOCK), BLOCK)])
        pre = dot3(xs, ws, NN)
        sig = jax.nn.sigmoid(pre)
        val = pre * sig
        act[h] = val
        dsilu[h] = sig * (1.0 + pre * (1.0 - sig))
        u, v = val[:, 0:64], val[:, 64:128]
        q, k = val[:, 128:192], val[:, 192:256]
        score = dot3(halves(q), halves(k), NT) * scale
        ssig = jax.nn.sigmoid(score)
        a = score * ssig * mask
        attn[h] = a
        dsfac[h] = mask * (ssig * (1.0 + score * (1.0 - ssig))) * scale
        o = dot3(halves(a), halves(v), NN)
        outv[h] = o
        wos = halves(wo_ref[pl.ds(pl.multiple_of(h * HEAD_DIM, HEAD_DIM), HEAD_DIM), :])
        dz = dot3(gs, wos, NT)
        dzs[h] = dz
        dn = dz * u
        return (sums[0] + o, sums[1] + o * o, sums[2] + dn, sums[3] + dn * o)

    zero = jnp.zeros((count, HEAD_DIM), F32)
    sums = lax.fori_loop(0, heads, forward, (zero, zero, zero, zero))
    lane = lax.broadcasted_iota(jnp.int32, (count, 128), 1)
    packed = jnp.zeros((count, 128), F32)
    for i in range(4):
        packed = jnp.where(lane == i, jnp.sum(sums[i], axis=1, keepdims=True), packed)
    stat[...] = packed.T[0:8]
    pl.semaphore_wait(barrier, len(partners))

    def stat_to(k):
        return remote(stat, stat_in.at[k], ms.at[0, k], mr.at[0, k], at_mp[k])

    for k in range(n_mp - 1):
        stat_to(k).start()
    loads[5].wait()
    loads[6].wait()
    x_t = x_ref[...].T
    xt_hi[...], xt_lo[...] = halves(x_t)
    place = lax.broadcasted_iota(jnp.int32, (rows, count), 0)
    inner = n_z * n_mp * own
    pc, px = place // (2 * inner), (place // inner) % 2
    pz, pm = (place // (n_mp * own)) % n_z, place % (n_mp * own)
    wanted = ((pz * 2 + px) * 2 + pc) * (n_mp * own) + pm
    hits = jnp.where(wanted == ids_ref[...], 1.0, 0.0).astype(BF16)
    sl[...] = (dot(hits, gs[0], NN) + dot(hits, gs[1], NN)) * (1.0 / n_mp)

    total = stat[...]
    for k in range(n_mp - 1):
        stat_to(k).wait()
        total = total + stat_in[k]
    cols = jnp.concatenate([total, jnp.zeros((120, count), F32)], axis=0).T
    mean = cols[:, 0:1] / width
    var = cols[:, 1:2] / width - mean * mean
    rstd = lax.rsqrt(var + 1e-05)
    m1 = cols[:, 2:3] / width
    m2 = rstd * (cols[:, 3:4] - mean * cols[:, 2:3]) / width

    z_all = jnp.concatenate(
        [(outv[h] - mean) * rstd * act[h][:, 0:64] for h in range(heads)], axis=1
    )
    wo_grad = dot3(halves(z_all), gs, TN)
    if fuse:
        buf[0, 0:half] = wo_grad[:, 0:BLOCK]
        buf[0, half : 2 * half] = wo_grad[:, BLOCK : 2 * BLOCK]
        stage(0, 0)
        wopart_ref[...] = jnp.zeros(wopart_ref.shape, F32)
    else:
        wopart_ref[...] = wo_grad

    def backward(h, carry):
        val = act[h]
        u, v = val[:, 0:64], val[:, 64:128]
        q, k = val[:, 128:192], val[:, 192:256]
        nrm = (outv[h] - mean) * rstd
        dz = dzs[h]
        dn = dz * u
        du = dz * nrm
        do = halves(rstd * (dn - m1 - nrm * m2))
        da = dot3(do, halves(v), NT)
        dv = dot3(halves(attn[h]), do, TN)
        ds = halves(da * dsfac[h])
        dq = dot3(ds, halves(k), NN)
        dk = dot3(ds, halves(q), TN)
        dpre = halves(jnp.concatenate([du, dv, dq, dk], axis=1) * dsilu[h])
        buf[h + off] = dot3((xt_hi[...], xt_lo[...]), dpre, NN)
        stage(0, h + off)
        rowsum = dot(hits, dpre[0], NN) + dot(hits, dpre[1], NN)
        ws = halves(w_ref[:, pl.ds(pl.multiple_of(h * BLOCK, BLOCK), BLOCK)])
        sl[...] += dot3(halves(rowsum), ws, NT)
        for s in range(1, min(6, heads - 1 + off) + 1):
            if off == 1 and s == 1:
                stage(s, h)
            else:
                pl.when(h + off - s >= 0)(functools.partial(stage, s, h + off - s))
        return carry

    lax.fori_loop(0, heads, backward, 0)

    s_half, s_q = rows // 2, rows // 4
    s_mine = span(c * s_half + x * s_q, s_q)

    def sl_core():
        return remote(sl.at[span((1 - c) * s_half, s_half)], slc, ls.at[0], lr.at[0], at_core)

    def sl_x():
        return remote(sl.at[span(c * s_half + (1 - x) * s_q, s_q)], slx, ls.at[1], lr.at[1], at_x)

    def sl_z(k):
        return remote(sl.at[s_mine], slz.at[k], lzs.at[k], lzr.at[k], at_z[k])

    def sl_mp(k):
        return remote(slq, slm.at[k], ms.at[1, k], mr.at[1, k], at_mp[k])

    def slab(t):
        if t == 0:
            sl_core().start()
        elif t == 1:
            sl_core().wait()
            sl[span(c * s_half, s_half)] += slc[...]
            sl_x().start()
        elif t == 2:
            sl_x().wait()
            sl[s_mine] += slx[...]
            for k in range(n_z - 1):
                sl_z(k).start()
        elif t == 3:
            part = sl[s_mine]
            for k in range(n_z - 1):
                sl_z(k).wait()
                part = part + slz[k]
            slq[...] = part
            for k in range(n_mp - 1):
                sl_mp(k).start()
        elif t == 4:
            part = slq[pl.ds((z * n_mp + mp) * own, own), :]
            for k in range(n_mp - 1):
                sl_mp(k).wait()
                part = part + slm[k, pl.ds((z * n_mp + mp) * own, own), :]
            newa = accum_ref[...] + jnp.sum(part * part, axis=1, keepdims=True) / width
            newa_ref[...] = newa
            newt_ref[...] = table_ref[...] - 0.5 * part * lax.rsqrt(newa)

    slab(0)
    for t in range(1, 7):
        tick = heads - 1 + off + t
        for s in range(0, 7):
            if 0 <= tick - s < pieces:
                stage(s, tick - s)
        slab(t)
    for p in range(pieces):
        keep(p).wait()


def layout_kernel(off, pieces_ref, table_ref, *refs):
    held, row, in_sem, sem = refs[-4:]
    w_ref, newt_ref = refs[0], refs[1]
    count = held.shape[0]
    loads = [pltpu.make_async_copy(pieces_ref.at[p], held.at[p], in_sem.at[p]) for p in range(count)]
    loads.append(pltpu.make_async_copy(table_ref, row, in_sem.at[count]))
    for load in loads:
        load.start()
    moves = []
    for p in range(count):
        if p < off:
            tokens = refs[2].shape[0]
            moves.append([
                (held.at[p, pl.ds(i * tokens, tokens)], refs[2].at[:, pl.ds(i * BLOCK, BLOCK)]) for i in range(2)
            ])
        else:
            moves.append([(held.at[p], w_ref.at[:, pl.ds((p - off) * BLOCK, BLOCK)])])
    moves.append([(row, newt_ref)])
    copies = []
    for load, after in zip(loads, moves):
        load.wait()
        for src, dst in after:
            copies.append(pltpu.make_async_copy(src, dst, sem.at[len(copies)]))
            copies[-1].start()
    for copy in copies:
        copy.wait()


def body(layer_input, grad_out, segment, item_ids, w_uvqk, w_out, table, accum):
    count, width = layer_input.shape
    cols = w_uvqk.shape[1]
    heads = cols // BLOCK
    feats = heads * HEAD_DIM
    n_dp, n_mp = lax.axis_size("dp"), lax.axis_size("mp")
    own = table.shape[0]
    rows = own * n_dp * n_mp
    n_z = n_dp // 4
    fuse = feats == BLOCK
    pieces = heads + (1 if fuse else 0)
    half, quarter = width // 2, width // 4
    chunk = quarter // n_z
    wo_shape = (8, 128) if fuse else (feats, width)
    vmem = pl.BlockSpec(memory_space=pltpu.VMEM)
    hbm = pl.BlockSpec(memory_space=pl.ANY)
    dma = pltpu.SemaphoreType.DMA
    out, wo_part, new_table, new_accum = pl.pallas_call(
        functools.partial(kernel, n_z, n_mp, fuse),
        out_shape=(
            jax.ShapeDtypeStruct((pieces, width, BLOCK), F32),
            jax.ShapeDtypeStruct(wo_shape, F32),
            jax.ShapeDtypeStruct((own, width), F32),
            jax.ShapeDtypeStruct((own, 1), F32),
        ),
        in_specs=[hbm] * 7 + [vmem],
        out_specs=(hbm, vmem, vmem, vmem),
        scratch_shapes=[
            pltpu.VMEM((count, width), F32),
            pltpu.VMEM((count, width), F32),
            pltpu.VMEM((1, count), jnp.int32),
            pltpu.VMEM((1, count), jnp.int32),
            pltpu.VMEM((width, cols), F32),
            pltpu.VMEM((feats, width), F32),
            pltpu.VMEM((own, width), F32),
            dma((7,)),
            dma((pieces,)),
            pltpu.VMEM((pieces, width, BLOCK), F32),
            pltpu.VMEM((pieces, width, BLOCK), F32),
            pltpu.VMEM((width, count), BF16),
            pltpu.VMEM((width, count), BF16),
            pltpu.VMEM((heads, count, BLOCK), F32),
            pltpu.VMEM((heads, count, BLOCK), F32),
            pltpu.VMEM((heads, count, count), F32),
            pltpu.VMEM((heads, count, count), F32),
            pltpu.VMEM((heads, count, HEAD_DIM), F32),
            pltpu.VMEM((heads, count, HEAD_DIM), F32),
            pltpu.VMEM((8, count), F32),
            pltpu.VMEM((n_mp - 1, 8, count), F32),
            pltpu.VMEM((pieces, half, BLOCK), F32),
            pltpu.VMEM((pieces, quarter, BLOCK), F32),
            pltpu.VMEM((pieces, n_z - 1, chunk, BLOCK), F32),
            pltpu.VMEM((rows, width), F32),
            pltpu.VMEM((rows // 2, width), F32),
            pltpu.VMEM((rows // 4, width), F32),
            pltpu.VMEM((n_z - 1, rows // 4, width), F32),
            pltpu.VMEM((rows // 4, width), F32),
            pltpu.VMEM((n_mp - 1, rows // 4, width), F32),
            dma((4, pieces)),
            dma((4, pieces)),
            dma((pieces, n_z)),
            dma((pieces, n_z)),
            dma((2, pieces, n_z - 1)),
            dma((2, pieces, n_z - 1)),
            dma((2,)),
            dma((2,)),
            dma((n_z - 1,)),
            dma((n_z - 1,)),
            dma((2, n_mp - 1)),
            dma((2, n_mp - 1)),
        ],
        compiler_params=pltpu.CompilerParams(
            collective_id=0, has_side_effects=True, vmem_limit_bytes=56 * 1024 * 1024
        ),
    )(
        layer_input,
        grad_out,
        segment,
        item_ids.reshape(1, count),
        w_uvqk,
        w_out,
        table,
        accum.reshape(own, 1),
    )
    results = [
        jax.ShapeDtypeStruct((width, cols), F32),
        jax.ShapeDtypeStruct((own, width), F32),
    ] + ([jax.ShapeDtypeStruct((feats, width), F32)] if fuse else [])
    laid = pl.pallas_call(
        functools.partial(layout_kernel, 1 if fuse else 0),
        out_shape=tuple(results),
        in_specs=[hbm] * 2,
        out_specs=(hbm,) * len(results),
        scratch_shapes=[
            pltpu.VMEM((pieces, width, BLOCK), F32),
            pltpu.VMEM((own, width), F32),
            dma((pieces + 1,)),
            dma((heads + 3,)),
        ],
        compiler_params=pltpu.CompilerParams(vmem_limit_bytes=56 * 1024 * 1024),
    )(out, new_table)
    w_uvqk_grad, new_table = laid[:2]
    w_out_grad = laid[2] if fuse else lax.psum(wo_part, "dp")
    return w_uvqk_grad, w_out_grad, new_table, new_accum.reshape(own)


def solution(mesh):
    placed = (
        P("dp", None),
        P("dp", None),
        P("dp", None),
        P("dp"),
        P(None, "mp"),
        P("mp", None),
        P(("dp", "mp"), None),
        P(("dp", "mp")),
    )
    return jax.shard_map(
        body,
        mesh=mesh,
        in_specs=placed,
        out_specs=(P(None, "mp"), P("mp", None), P(("dp", "mp"), None), P(("dp", "mp"))),
        check_vma=False,
    )
```
